128 devices in a mesh: queue: 16 (over x_hi, z, core), tok: 8 (over x_lo, y).
Axes of the slice: x: 4 (x_hi: 2, x_lo: 2; x = x_hi * 2 + x_lo), y: 4, z: 4, core: 2. Of those that a mesh axis runs over, the one named last changes fastest.
Arguments:
- latents: float32 [16, 1024, 64], P('queue', 'tok'), may hold values from -6 to 6
- step_index: int32 [16], replicated, may hold values from 0 to 63, as said below
- tail_noise: float32 [1024, 64], P('tok'), may hold values from -6 to 6
- patch_weight: bfloat16 [64, 1536], replicated, may hold values from -0.75 to 0.75
- time_table: float32 [64, 3, 1536], replicated, may hold values from -3 to 3
- qkv_weight: bfloat16 [1536, 4608], replicated, may hold values from -1 to 1
- q_gain: float32 [1536], replicated, may hold values from 1 to 3
- k_gain: float32 [1536], replicated, may hold values from 1 to 3
- out_weight: bfloat16 [1536, 1536], replicated, may hold values from -0.15625 to 0.15625
- head_weight: bfloat16 [1536, 64], replicated, may hold values from -0.15625 to 0.15625
Outputs:
- velocity: float32 [16, 1024, 64], P('queue', 'tok')
- queue_next: float32 [16, 1024, 64], P('queue', 'tok')
- leaving: float32 [64, 1024], P('queue', 'tok')
The draws below stay inside these ranges and needn't reach their ends.
Inputs may be any that keep to these rules, and one draw needn't show every extreme that they name: `step_index`: strictly rising along the queue, by 1 to 4 from one frame to the next; the tail frame is at level 63.
All inputs are finite; a program needn't handle non-finite values.
Results may differ from the reference program's by a relative error of at most 0.0095.
Values may be sent and summed in bfloat16 or wider, within the bound.
A program may use at most 320 MiB of HBM per device.

```python
import math
import jax
import jax.numpy as jnp
from jax import lax

D = 1536
HEADS = 12
HEAD_DIM = 128
C = 64
FRAMES = 16
TOKF = 1024
LEVELS = 64


def draw_step_index(key, part):
    strides = jax.random.randint(jax.random.fold_in(key, 12), (FRAMES - 1,), 1, 5).astype(jnp.int32)
    opening = (LEVELS - 1 - jnp.sum(strides)).astype(jnp.int32)
    rising = jnp.concatenate([jnp.zeros((1,), jnp.int32), jnp.cumsum(strides).astype(jnp.int32)])
    return (opening + rising).astype(jnp.int32)


def draw_qkv_weight(key, part):
    base = jax.random.normal(jax.random.fold_in(key, 21), (D, 3 * D), jnp.float32) * D ** (-0.5)
    base = jnp.clip(base, -1.0, 1.0)
    return base.astype(jnp.bfloat16)


def level_of(own_key, shape, cuts, low, top_value):
    gain, own = 1.0, jax.random.fold_in(own_key, 6)
    for position, parts in cuts:
        draws = jnp.exp(jax.random.uniform(jax.random.fold_in(own, position), (parts,), jnp.float32, low / len(cuts), top_value / len(cuts)))
        gain = gain * jnp.repeat(draws, shape[position] // parts).reshape([-1 if axis == position else 1 for axis in range(len(shape))])
    return gain


def gaussian(own_key, dims, width, bound, split=(), kind=jnp.bfloat16):
    entries = jax.random.normal(own_key, dims, jnp.float32) * width
    if len(split) > 0:
        entries = level_of(own_key, dims, split, -0.22, 0.18) * entries
    return jnp.clip(entries, min=-bound, max=bound).astype(kind)


def setup_inputs(seed: int = 0) -> dict:
    key_list = jax.random.split(jax.random.key(seed), 11)
    latents = gaussian(key_list[0], (FRAMES, TOKF, C), 1.0, 6.0, ((0, 16), (1, 8)), jnp.float32)
    step_index = draw_step_index(jax.random.fold_in(key_list[10], 71), 0)
    tail_noise = gaussian(key_list[2], (TOKF, C), 1.0, 6.0, ((0, 8),), jnp.float32)
    patch_weight = gaussian(key_list[3], (C, D), C ** -0.5, 0.75)
    time_table = gaussian(key_list[4], (LEVELS, 3, D), 0.5, 3.0, (), jnp.float32)
    qkv_weight = draw_qkv_weight(jax.random.fold_in(key_list[10], 71), 0)
    q_gain = jnp.clip(jnp.exp(jax.random.uniform(key_list[6], (D,), jnp.float32, math.log(1.0), math.log(3.0))), 1.0, 3.0)
    k_gain = jnp.clip(jnp.exp(jax.random.uniform(key_list[7], (D,), jnp.float32, math.log(1.0), math.log(3.0))), 1.0, 3.0)
    out_weight = gaussian(key_list[8], (D, D), D ** -0.5, 0.15625)
    head_weight = gaussian(key_list[9], (D, C), D ** -0.5, 0.15625)
    return dict(latents=latents, step_index=step_index, tail_noise=tail_noise, patch_weight=patch_weight, time_table=time_table, qkv_weight=qkv_weight, q_gain=q_gain, k_gain=k_gain, out_weight=out_weight, head_weight=head_weight)


def layer_norm(values):
    mean_row = lax.optimization_barrier(jnp.mean(values, axis=-1, keepdims=True))
    centred = values - mean_row
    variance = lax.optimization_barrier(jnp.mean(centred * centred, axis=-1, keepdims=True))
    return centred * lax.rsqrt(variance + 1e-06)

def rms_norm(values, gain_vec):
    return values * lax.rsqrt(lax.optimization_barrier(jnp.mean(values * values, axis=-1, keepdims=True)) + 1e-06) * gain_vec

def widen(values):
    return lax.optimization_barrier(values).astype(jnp.float32)

def reference(latents, step_index, tail_noise, patch_weight, time_table, qkv_weight, q_gain, k_gain, out_weight, head_weight):
    one_hot = (step_index[:, None] == jnp.arange(LEVELS, dtype=jnp.int32)[None, :]).astype(jnp.float32)
    modulation = jnp.dot(one_hot, time_table.reshape(LEVELS, 3 * D), precision=lax.Precision.HIGHEST).reshape(FRAMES, 3, D)
    shift_vec = modulation[:, 0][:, None, :]
    scale_vec = modulation[:, 1][:, None, :]
    gate_vec = modulation[:, 2][:, None, :]
    hidden = jnp.dot(latents.reshape(FRAMES * TOKF, C).astype(jnp.bfloat16), patch_weight, preferred_element_type=jnp.float32).reshape(FRAMES, TOKF, D)
    normed = (layer_norm(hidden) * (1.0 + scale_vec) + shift_vec).astype(jnp.bfloat16)
    projected = jnp.dot(normed.reshape(FRAMES * TOKF, D), qkv_weight, preferred_element_type=jnp.float32)
    queries = rms_norm(projected[:, :D], q_gain).astype(jnp.bfloat16).reshape(FRAMES, TOKF, HEADS, HEAD_DIM)
    key_rows = rms_norm(projected[:, D:2 * D], k_gain).astype(jnp.bfloat16).reshape(FRAMES * TOKF, HEADS, HEAD_DIM)
    value_rows = projected[:, 2 * D:].astype(jnp.bfloat16).reshape(FRAMES * TOKF, HEADS, HEAD_DIM)
    all_keys = widen(key_rows)
    all_values = widen(value_rows)

    def one_frame(frame_idx):
        own_queries = widen(lax.dynamic_index_in_dim(queries, frame_idx, 0, keepdims=False))
        scores = jnp.einsum('qhd,khd->qhk', own_queries, all_keys) * HEAD_DIM ** (-0.5)
        weights = jnp.exp(scores - lax.optimization_barrier(jnp.max(scores, axis=-1, keepdims=True)))
        totals = lax.optimization_barrier(jnp.sum(weights, axis=-1))
        rounded = widen(weights.astype(jnp.bfloat16))
        attended = jnp.einsum('qhk,khd->qhd', rounded, all_values) / totals[..., None]
        return attended.reshape(TOKF, D).astype(jnp.bfloat16)
    attended = lax.map(one_frame, jnp.arange(FRAMES, dtype=jnp.int32))
    attn_out = jnp.dot(attended.reshape(FRAMES * TOKF, D), out_weight, preferred_element_type=jnp.float32).reshape(FRAMES, TOKF, D)
    residual = hidden + gate_vec * attn_out
    velocity = jnp.dot(residual.reshape(FRAMES * TOKF, D).astype(jnp.bfloat16), head_weight, preferred_element_type=jnp.float32).reshape(FRAMES, TOKF, C)
    level_before = jnp.concatenate([jnp.full((1,), -1, jnp.int32), step_index[:-1]])
    sigma_now = (step_index.astype(jnp.float32) + 1.0) / LEVELS
    sigma_next = (level_before.astype(jnp.float32) + 1.0) / LEVELS
    updated = latents + (sigma_next - sigma_now)[:, None, None] * velocity
    queue_next = jnp.concatenate([updated[1:], tail_noise[None]], axis=0)
    leaving = updated[0].T
    return (velocity, queue_next, leaving)
```

```python
import jax
import jax.numpy as jnp
from jax import lax
from jax.experimental import pallas as pl
from jax.experimental.pallas import tpu as pltpu
from jax.sharding import PartitionSpec as P

HEAD_DIM = 128
LOG2E = 1.4426950408889634
SAFE_LOG2 = 112.0
VALUE_SHRINK = 0.0625
MESH_ID = pl.DeviceIdType.MESH


def sent_together(arrays, axis, split_dim, concat_dim, along):
    columns = [a.reshape(*a.shape[:along], -1) for a in arrays]
    both = jnp.concatenate(columns, axis=along)
    filled, at, outs = (
        lax.all_to_all(both, axis, split_axis=split_dim, concat_axis=concat_dim, tiled=True),
        0,
        [],
    )
    for a, column in zip(arrays, columns):
        slab = filled[..., at : at + column.shape[along]]
        outs.append(slab.reshape(*slab.shape[:along], *a.shape[along:]))
        at += column.shape[along]
    return tuple(outs)


def passed_along(value, axis, by):
    peers = lax.axis_size(axis)
    pairs = [(i, i + by) for i in range(peers) if 0 <= i + by < peers]
    return lax.ppermute(value, axis, pairs)


def picked(value, axis, root):
    return lax.dynamic_index_in_dim(lax.all_gather(value, axis), root, 0, keepdims=False)


def layer_norm(values):
    mean_row = jnp.mean(values, axis=-1, keepdims=True)
    centred = values - mean_row
    variance = jnp.mean(centred * centred, axis=-1, keepdims=True)
    return centred * lax.rsqrt(variance + 1e-06)


def rms_norm(values, gain_vec):
    return values * lax.rsqrt(jnp.mean(values * values, axis=-1, keepdims=True) + 1e-06) * gain_vec


def fold_keys(carried, queries, portion, scaling):
    run_max, run_sum, run_out = carried
    head_count = queries.shape[1]
    head_size = queries.shape[2]
    feature = head_count * head_size
    key_rows = portion[:, :feature].reshape(portion.shape[0], head_count, head_size)
    value_rows = portion[:, feature:].reshape(portion.shape[0], head_count, head_size)
    scores = (
        jnp.einsum("rhd,khd->rhk", queries, key_rows, preferred_element_type=jnp.float32) * scaling
    )
    new_max = jnp.maximum(run_max, jnp.max(scores, axis=-1))
    weights = jnp.exp(scores - new_max[..., None])
    run_sum = jnp.sum(weights, axis=-1)
    run_out = jnp.einsum(
        "rhk,khd->rhd", weights.astype(jnp.bfloat16), value_rows, preferred_element_type=jnp.float32
    )
    return (new_max, run_sum, run_out)


def merge_states(maxima, totals, outputs):
    top = jnp.max(maxima, axis=0)
    factor = jnp.exp(maxima - top[None])
    return (top, jnp.sum(totals * factor, axis=0), jnp.sum(outputs * factor[..., None], axis=0))


def fresh_state(row_count, head_count, head_size):
    return (
        jnp.full((row_count, head_count), -1e30, jnp.float32),
        jnp.zeros((row_count, head_count), jnp.float32),
        jnp.zeros((row_count, head_count, head_size), jnp.float32),
    )


def key_value_rows(normed, qkv_weight, k_gain, feature):
    projected = jnp.dot(normed, qkv_weight[:, feature:], preferred_element_type=jnp.float32)
    key_part = rms_norm(projected[:, :feature], k_gain).astype(jnp.bfloat16)
    return jnp.concatenate([key_part, projected[:, feature:].astype(jnp.bfloat16)], axis=1)


def careful(
    latents,
    step_index,
    tail_noise,
    patch_weight,
    time_table,
    qkv_weight,
    q_gain,
    k_gain,
    out_weight,
    head_weight,
):
    feature = patch_weight.shape[1]
    head_size = HEAD_DIM
    head_count = feature // head_size
    scaling = head_size ** (-0.5)
    levels = time_table.shape[0]
    frames = lax.axis_size("queue")
    position = lax.axis_index("queue")
    latent = latents[0]
    tok_rows = latent.shape[0]
    level_now = step_index[position]
    level_before = jnp.where(position > 0, step_index[jnp.maximum(position - 1, 0)], -1)
    one_hot = (jnp.arange(levels, dtype=jnp.int32) == level_now).astype(jnp.float32)[None, :]
    modulation = jnp.dot(
        one_hot, time_table.reshape(levels, 3 * feature), precision=lax.Precision.HIGHEST
    ).reshape(3, feature)
    hidden = jnp.dot(latent.astype(jnp.bfloat16), patch_weight, preferred_element_type=jnp.float32)
    normed = (layer_norm(hidden) * (1.0 + modulation[1]) + modulation[0]).astype(jnp.bfloat16)
    query_proj = jnp.dot(normed, qkv_weight[:, :feature], preferred_element_type=jnp.float32)
    queries = rms_norm(query_proj, q_gain).astype(jnp.bfloat16)
    key_value = key_value_rows(normed, qkv_weight, k_gain, feature)
    whole_queries = lax.all_gather(queries, "tok", axis=0, tiled=True)
    frame_rows = whole_queries.shape[0]
    whole_queries = whole_queries.reshape(frame_rows, head_count, head_size)
    state = fold_keys(
        fresh_state(frame_rows, head_count, head_size),
        whole_queries,
        lax.all_gather(key_value, "queue", axis=0, tiled=True),
        scaling,
    )
    parts = tuple(
        (
            part.astype(jnp.float32)
            for part in sent_together(
                (
                    state[0][None].astype(jnp.bfloat16),
                    state[1][None].astype(jnp.bfloat16),
                    state[2][None].astype(jnp.bfloat16),
                ),
                "tok",
                1,
                0,
                3,
            )
        )
    )
    carried = merge_states(parts[0], parts[1], parts[2])
    run_max, run_sum, run_out = carried
    attended = (run_out / run_sum[..., None]).reshape(tok_rows, feature).astype(jnp.bfloat16)
    attn_out = jnp.dot(attended, out_weight, preferred_element_type=jnp.float32)
    residual = hidden + modulation[2] * attn_out
    velocity = jnp.dot(
        residual.astype(jnp.bfloat16), head_weight, preferred_element_type=jnp.float32
    )
    sigma_now = (level_now.astype(jnp.float32) + 1.0) / levels
    sigma_next = (level_before.astype(jnp.float32) + 1.0) / levels
    updated = latent + (sigma_next - sigma_now) * velocity
    arrived = passed_along(updated.astype(jnp.bfloat16), "queue", -1).astype(updated.dtype)
    queue_next = jnp.where(position == frames - 1, tail_noise, arrived)
    clean_frame = picked(updated.T.astype(jnp.bfloat16), "queue", 0).astype(jnp.float32)
    channel_share = clean_frame.shape[0] // frames
    leaving = lax.dynamic_slice_in_dim(clean_frame, position * channel_share, channel_share, 0)
    return (velocity[None], queue_next[None], leaving)


def dot_nt(a, b):
    return lax.dot_general(a, b, (((1,), (1,)), ((), ())), preferred_element_type=jnp.float32)


def attention_kernel(q_in, kv_in, out, q_all, kv_all, o_send, o_recv, a_send,
                     xq_s, xq_r, xk_s, xk_r, yq_s, yq_r, zk_s, zk_r, ck_s, ck_r,
                     oy_s, oy_r, ox_s, ox_r):
    queue = lax.axis_index("queue")
    tok = lax.axis_index("tok")
    core = lax.rem(queue, 2)
    z = lax.rem(queue // 2, 4)
    x = (queue // 8) * 2 + tok // 4
    y = lax.rem(tok, 4)

    def device(px, py, pz, pc):
        return (((px // 2) * 4 + pz) * 2 + pc, lax.rem(px, 2) * 4 + py)

    def hop(v, d):
        return lax.rem(v + d + 4, 4)

    slot = z * 2 + core

    def rows(n, size):
        return pl.ds(pl.multiple_of(n * size, size), size)

    def remote(src, dst, s, r, dev):
        return pltpu.make_async_remote_copy(src_ref=src, dst_ref=dst, send_sem=s, recv_sem=r,
                                            device_id=dev, device_id_type=MESH_ID)

    def x_query(h, d):
        g = hop(x, d)
        return remote(q_in.at[g * 3 + h], q_all.at[h, y, rows(x, 128)],
                      xq_s.at[h, d], xq_r.at[h, d], device(g, y, z, core))

    def x_query_in(h, d):
        g = hop(x, -d)
        return remote(q_in.at[x * 3 + h], q_all.at[h, y, rows(g, 128)],
                      xq_s.at[h, d], xq_r.at[h, d], device(g, y, z, core))

    def x_keys(h, d):
        g = hop(x, d)
        return remote(kv_in.at[g * 3 + h], kv_all.at[h, :, rows(slot * 4 + x, 128)],
                      xk_s.at[h, d], xk_r.at[h, d], device(g, y, z, core))

    def x_keys_in(h, d):
        g = hop(x, -d)
        return remote(kv_in.at[x * 3 + h], kv_all.at[h, :, rows(slot * 4 + g, 128)],
                      xk_s.at[h, d], xk_r.at[h, d], device(g, y, z, core))

    def y_query(h, d):
        return remote(q_all.at[h, y], q_all.at[h, y], yq_s.at[h, d], yq_r.at[h, d],
                      device(x, hop(y, d), z, core))

    def y_query_in(h, d):
        g = hop(y, -d)
        return remote(q_all.at[h, g], q_all.at[h, g], yq_s.at[h, d], yq_r.at[h, d],
                      device(x, g, z, core))

    def z_keys(h, d):
        at = kv_all.at[h, :, rows(slot, 512)]
        return remote(at, at, zk_s.at[h, d], zk_r.at[h, d], device(x, y, hop(z, d), core))

    def z_keys_in(h, d):
        g = hop(z, -d)
        at = kv_all.at[h, :, rows(g * 2 + core, 512)]
        return remote(at, at, zk_s.at[h, d], zk_r.at[h, d], device(x, y, g, core))

    def c_keys(h, d):
        at = kv_all.at[h, :, rows(hop(z, -d) * 2 + core, 512)]
        return remote(at, at, ck_s.at[h, d], ck_r.at[h, d], device(x, y, z, 1 - core))

    def c_keys_in(h, d):
        at = kv_all.at[h, :, rows(hop(z, -d) * 2 + 1 - core, 512)]
        return remote(at, at, ck_s.at[h, d], ck_r.at[h, d], device(x, y, z, 1 - core))

    def y_part(h, d):
        return remote(o_send.at[h, hop(y, d)], o_recv.at[h, y], oy_s.at[h, d], oy_r.at[h, d],
                      device(x, hop(y, d), z, core))

    def y_part_in(h, d):
        g = hop(y, -d)
        return remote(o_send.at[h, g], o_recv.at[h, g], oy_s.at[h, d], oy_r.at[h, d],
                      device(x, g, z, core))

    def x_back(h, d):
        g = hop(x, d)
        return remote(a_send.at[h, g], out.at[x * 3 + h], ox_s.at[h, d], ox_r.at[h, d],
                      device(g, y, z, core))

    def x_back_in(h, d):
        g = hop(x, -d)
        return remote(a_send.at[h, g], out.at[g * 3 + h], ox_s.at[h, d], ox_r.at[h, d],
                      device(g, y, z, core))

    barrier = pltpu.get_barrier_semaphore()
    for d in (1, 2, 3):
        for dev in (device(hop(x, d), y, z, core), device(x, hop(y, d), z, core),
                    device(x, y, hop(z, d), core)):
            pl.semaphore_signal(barrier, inc=1, device_id=dev, device_id_type=MESH_ID)
    pl.semaphore_signal(barrier, inc=1, device_id=device(x, y, z, 1 - core),
                        device_id_type=MESH_ID)
    pl.semaphore_wait(barrier, 10)

    for h in range(3):
        for d in (1, 3, 2):
            x_keys(h, d).start()
        for d in (1, 3, 2):
            x_query(h, d).start()
    for h in range(3):
        q_all[h, y, rows(x, 128), :] = q_in[x * 3 + h]
        for kv in range(2):
            kv_all[h, kv, rows(slot * 4 + x, 128), :] = kv_in[x * 3 + h, kv]

    def spread(h):
        for d in (1, 3, 2):
            x_keys_in(h, d).wait_recv()
        for d in (1, 3, 2):
            z_keys(h, d).start()
        c_keys(h, 0).start()
        for d in (1, 3, 2):
            x_query_in(h, d).wait_recv()
        for d in (1, 3, 2):
            y_query(h, d).start()

    def share(h, d):
        z_keys_in(h, d).wait_recv()
        c_keys(h, d).start()

    for h in range(3):
        spread(h)
    for d in (1, 3, 2):
        share(0, d)
    for d in (0, 1, 3, 2):
        c_keys_in(0, d).wait_recv()

    def combine(h):
        for d in (1, 2, 3):
            y_part_in(h, d).wait_recv()
        parts = [o_send.at[h, y]] + [o_recv.at[h, hop(y, d)] for d in (1, 2, 3)]
        den = jnp.zeros((4, 128), jnp.float32)
        for part in parts:
            tail = part[512:528, :].astype(jnp.float32)
            den = den + (tail[0:4] + tail[4:8])
        inv = (1.0 / VALUE_SHRINK) / den
        for g in range(4):
            num = parts[0][g * 128:(g + 1) * 128, :].astype(jnp.float32)
            for part in parts[1:]:
                num = num + part[g * 128:(g + 1) * 128, :].astype(jnp.float32)
            column = jnp.transpose(jnp.broadcast_to(inv[g:g + 1, :], (128, 128)))
            a_send[h, g] = (num * column).astype(jnp.bfloat16)
        out[x * 3 + h] = a_send[h, x]
        for d in (1, 3, 2):
            x_back(h, d).start()

    def chunk(t, carry):
        h, i = t // 4, lax.rem(t, 4)
        to = lax.rem(y + i + 1, 4)

        @pl.when(i < 3)
        def _():
            y_query_in(h, 3 - i).wait_recv()

        queries = q_all[h, to]
        scores = dot_nt(queries, kv_all[h, 0])
        weights = jnp.exp2(scores)
        total = weights[:, 0:128]
        for n in range(1, 32):
            total = total + weights[:, n * 128:(n + 1) * 128]
        num = jnp.dot(weights.astype(jnp.bfloat16), kv_all[h, 1],
                      preferred_element_type=jnp.float32)
        o_send[h, to, 0:512, :] = num.astype(jnp.bfloat16)
        rows_of = [jnp.sum(jnp.transpose(total[g * 128:(g + 1) * 128, :]), axis=0, keepdims=True)
                   for g in range(4)]
        den = jnp.concatenate(rows_of, axis=0)
        high = den.astype(jnp.bfloat16).astype(jnp.float32)
        tail = jnp.concatenate([high, den - high, jnp.zeros((8, 128), jnp.float32)], axis=0)
        o_send[h, to, 512:528, :] = tail.astype(jnp.bfloat16)

        @pl.when(i < 3)
        def _():
            y_part(h, i + 1).start()

        @pl.when(jnp.logical_and(h < 2, i == 1))
        def _():
            share(h + 1, 1)
            share(h + 1, 3)

        @pl.when(jnp.logical_and(h < 2, i == 2))
        def _():
            share(h + 1, 2)

        @pl.when(jnp.logical_and(h < 2, i == 3))
        def _():
            for d in (0, 1, 3, 2):
                c_keys_in(h + 1, d).wait_recv()

        @pl.when(jnp.logical_and(h > 0, i == 1))
        def _():
            combine(h - 1)

        return carry

    lax.fori_loop(0, 12, chunk, 0)
    combine(2)
    for h in range(3):
        for d in (1, 3, 2):
            x_back_in(h, d).wait_recv()
    for h in range(3):
        for d in (1, 2, 3):
            x_keys(h, d).wait_send()
            x_query(h, d).wait_send()
            y_query(h, d).wait_send()
            z_keys(h, d).wait_send()
            y_part(h, d).wait_send()
            x_back(h, d).wait_send()
        for d in range(4):
            c_keys(h, d).wait_send()


def attention(q_in, kv_in):
    sems = [pltpu.SemaphoreType.DMA((3, 4))] * 14
    return pl.pallas_call(
        attention_kernel,
        out_shape=jax.ShapeDtypeStruct((12, 128, 128), jnp.bfloat16),
        in_specs=[pl.BlockSpec(memory_space=pltpu.VMEM)] * 2,
        out_specs=pl.BlockSpec(memory_space=pltpu.VMEM),
        scratch_shapes=[
            pltpu.VMEM((3, 4, 512, 128), jnp.bfloat16),
            pltpu.VMEM((3, 2, 4096, 128), jnp.bfloat16),
            pltpu.VMEM((3, 4, 528, 128), jnp.bfloat16),
            pltpu.VMEM((3, 4, 528, 128), jnp.bfloat16),
            pltpu.VMEM((3, 4, 128, 128), jnp.bfloat16),
        ] + sems,
        compiler_params=pltpu.CompilerParams(
            collective_id=1, has_side_effects=True, vmem_limit_bytes=56 * 2**20),
        cost_estimate=pl.CostEstimate(flops=13 * 10**9, bytes_accessed=20 * 10**6,
                                      transcendentals=25 * 10**6),
    )(q_in, kv_in)


def per_device(
    latents,
    step_index,
    tail_noise,
    patch_weight,
    time_table,
    qkv_weight,
    q_gain,
    k_gain,
    out_weight,
    head_weight,
):
    feature = patch_weight.shape[1]
    heads = feature // HEAD_DIM
    levels = time_table.shape[0]
    frames = lax.axis_size("queue")
    position = lax.axis_index("queue")
    latent = latents[0]
    level_now = step_index[position]
    level_before = jnp.where(position > 0, step_index[jnp.maximum(position - 1, 0)], -1)
    modulation = lax.dynamic_index_in_dim(time_table, level_now, 0, keepdims=False)
    hidden = jnp.dot(latent.astype(jnp.bfloat16), patch_weight, preferred_element_type=jnp.float32)
    normed = (layer_norm(hidden) * (1.0 + modulation[1]) + modulation[0]).astype(jnp.bfloat16)
    projected = jnp.dot(normed, qkv_weight, preferred_element_type=jnp.float32)
    scale = HEAD_DIM ** (-0.5) * LOG2E
    queries = (rms_norm(projected[:, :feature], q_gain) * scale).astype(jnp.bfloat16)
    keys = rms_norm(projected[:, feature:2 * feature], k_gain).astype(jnp.bfloat16)
    values = (projected[:, 2 * feature:] * VALUE_SHRINK).astype(jnp.bfloat16)

    def by_head(a):
        return a.reshape(-1, heads, HEAD_DIM).transpose(1, 0, 2)

    q_heads, k_heads, v_heads = by_head(queries), by_head(keys), by_head(values)

    def top_norm(a):
        wide = a.astype(jnp.float32)
        return jnp.max(jnp.sum(wide * wide, axis=-1), axis=-1)

    sizes = jnp.stack([top_norm(q_heads), top_norm(k_heads),
                       jnp.max(jnp.abs(v_heads.astype(jnp.float32)), axis=(1, 2))])
    sizes = lax.pmax(sizes, ("queue", "tok"))
    plain = jnp.logical_and(jnp.all(jnp.sqrt(sizes[0]) * jnp.sqrt(sizes[1]) <= SAFE_LOG2),
                            jnp.all(sizes[2] <= 2.0))
    attended = attention(q_heads, jnp.stack([k_heads, v_heads], axis=1))
    attended = attended.transpose(1, 0, 2).reshape(-1, feature)
    attn_out = jnp.dot(attended, out_weight, preferred_element_type=jnp.float32)
    residual = hidden + modulation[2] * attn_out
    velocity = jnp.dot(
        residual.astype(jnp.bfloat16), head_weight, preferred_element_type=jnp.float32
    )
    sigma_now = (level_now.astype(jnp.float32) + 1.0) / levels
    sigma_next = (level_before.astype(jnp.float32) + 1.0) / levels
    updated = latent + (sigma_next - sigma_now) * velocity
    arrived = passed_along(updated.astype(jnp.bfloat16), "queue", -1).astype(updated.dtype)
    queue_next = jnp.where(position == frames - 1, tail_noise, arrived)
    clean_frame = picked(updated.T.astype(jnp.bfloat16), "queue", 0).astype(jnp.float32)
    channel_share = clean_frame.shape[0] // frames
    leaving = lax.dynamic_slice_in_dim(clean_frame, position * channel_share, channel_share, 0)
    args = (latents, step_index, tail_noise, patch_weight, time_table, qkv_weight, q_gain,
            k_gain, out_weight, head_weight)
    return lax.cond(plain, lambda *_: (velocity[None], queue_next[None], leaving), careful, *args)


def solution(mesh):
    placed = (P("queue", "tok", None), P(), P("tok", None), P(), P(), P(), P(), P(), P(), P())
    return jax.shard_map(
        per_device,
        mesh=mesh,
        in_specs=placed,
        out_specs=(P("queue", "tok", None), P("queue", "tok", None), P("queue", "tok")),
        check_vma=False,
    )
```

```python
import jax
import jax.numpy as jnp
from jax import lax
from jax.experimental import pallas as pl
from jax.experimental.pallas import tpu as pltpu
from jax.sharding import PartitionSpec as P

HEAD_DIM = 128
LOG2E = 1.4426950408889634
SAFE_LOG2 = 112.0
VALUE_SHRINK = 0.0625
MESH_ID = pl.DeviceIdType.MESH


def sent_together(arrays, axis, split_dim, concat_dim, along):
    columns = [a.reshape(*a.shape[:along], -1) for a in arrays]
    both = jnp.concatenate(columns, axis=along)
    filled, at, outs = (
        lax.all_to_all(both, axis, split_axis=split_dim, concat_axis=concat_dim, tiled=True),
        0,
        [],
    )
    for a, column in zip(arrays, columns):
        slab = filled[..., at : at + column.shape[along]]
        outs.append(slab.reshape(*slab.shape[:along], *a.shape[along:]))
        at += column.shape[along]
    return tuple(outs)


def passed_along(value, axis, by):
    peers = lax.axis_size(axis)
    pairs = [(i, i + by) for i in range(peers) if 0 <= i + by < peers]
    return lax.ppermute(value, axis, pairs)


def picked(value, axis, root):
    return lax.dynamic_index_in_dim(lax.all_gather(value, axis), root, 0, keepdims=False)


def layer_norm(values):
    mean_row = jnp.mean(values, axis=-1, keepdims=True)
    centred = values - mean_row
    variance = jnp.mean(centred * centred, axis=-1, keepdims=True)
    return centred * lax.rsqrt(variance + 1e-06)


def rms_norm(values, gain_vec):
    return values * lax.rsqrt(jnp.mean(values * values, axis=-1, keepdims=True) + 1e-06) * gain_vec


def fold_keys(carried, queries, portion, scaling):
    run_max, run_sum, run_out = carried
    head_count = queries.shape[1]
    head_size = queries.shape[2]
    feature = head_count * head_size
    key_rows = portion[:, :feature].reshape(portion.shape[0], head_count, head_size)
    value_rows = portion[:, feature:].reshape(portion.shape[0], head_count, head_size)
    scores = (
        jnp.einsum("rhd,khd->rhk", queries, key_rows, preferred_element_type=jnp.float32) * scaling
    )
    new_max = jnp.maximum(run_max, jnp.max(scores, axis=-1))
    weights = jnp.exp(scores - new_max[..., None])
    run_sum = jnp.sum(weights, axis=-1)
    run_out = jnp.einsum(
        "rhk,khd->rhd", weights.astype(jnp.bfloat16), value_rows, preferred_element_type=jnp.float32
    )
    return (new_max, run_sum, run_out)


def merge_states(maxima, totals, outputs):
    top = jnp.max(maxima, axis=0)
    factor = jnp.exp(maxima - top[None])
    return (top, jnp.sum(totals * factor, axis=0), jnp.sum(outputs * factor[..., None], axis=0))


def fresh_state(row_count, head_count, head_size):
    return (
        jnp.full((row_count, head_count), -1e30, jnp.float32),
        jnp.zeros((row_count, head_count), jnp.float32),
        jnp.zeros((row_count, head_count, head_size), jnp.float32),
    )


def key_value_rows(normed, qkv_weight, k_gain, feature):
    projected = jnp.dot(normed, qkv_weight[:, feature:], preferred_element_type=jnp.float32)
    key_part = rms_norm(projected[:, :feature], k_gain).astype(jnp.bfloat16)
    return jnp.concatenate([key_part, projected[:, feature:].astype(jnp.bfloat16)], axis=1)


def careful(
    latents,
    step_index,
    tail_noise,
    patch_weight,
    time_table,
    qkv_weight,
    q_gain,
    k_gain,
    out_weight,
    head_weight,
):
    feature = patch_weight.shape[1]
    head_size = HEAD_DIM
    head_count = feature // head_size
    scaling = head_size ** (-0.5)
    levels = time_table.shape[0]
    frames = lax.axis_size("queue")
    position = lax.axis_index("queue")
    latent = latents[0]
    tok_rows = latent.shape[0]
    level_now = step_index[position]
    level_before = jnp.where(position > 0, step_index[jnp.maximum(position - 1, 0)], -1)
    one_hot = (jnp.arange(levels, dtype=jnp.int32) == level_now).astype(jnp.float32)[None, :]
    modulation = jnp.dot(
        one_hot, time_table.reshape(levels, 3 * feature), precision=lax.Precision.HIGHEST
    ).reshape(3, feature)
    hidden = jnp.dot(latent.astype(jnp.bfloat16), patch_weight, preferred_element_type=jnp.float32)
    normed = (layer_norm(hidden) * (1.0 + modulation[1]) + modulation[0]).astype(jnp.bfloat16)
    query_proj = jnp.dot(normed, qkv_weight[:, :feature], preferred_element_type=jnp.float32)
    queries = rms_norm(query_proj, q_gain).astype(jnp.bfloat16)
    key_value = key_value_rows(normed, qkv_weight, k_gain, feature)
    whole_queries = lax.all_gather(queries, "tok", axis=0, tiled=True)
    frame_rows = whole_queries.shape[0]
    whole_queries = whole_queries.reshape(frame_rows, head_count, head_size)
    state = fold_keys(
        fresh_state(frame_rows, head_count, head_size),
        whole_queries,
        lax.all_gather(key_value, "queue", axis=0, tiled=True),
        scaling,
    )
    parts = tuple(
        (
            part.astype(jnp.float32)
            for part in sent_together(
                (
                    state[0][None].astype(jnp.bfloat16),
                    state[1][None].astype(jnp.bfloat16),
                    state[2][None].astype(jnp.bfloat16),
                ),
                "tok",
                1,
                0,
                3,
            )
        )
    )
    carried = merge_states(parts[0], parts[1], parts[2])
    run_max, run_sum, run_out = carried
    attended = (run_out / run_sum[..., None]).reshape(tok_rows, feature).astype(jnp.bfloat16)
    attn_out = jnp.dot(attended, out_weight, preferred_element_type=jnp.float32)
    residual = hidden + modulation[2] * attn_out
    velocity = jnp.dot(
        residual.astype(jnp.bfloat16), head_weight, preferred_element_type=jnp.float32
    )
    sigma_now = (level_now.astype(jnp.float32) + 1.0) / levels
    sigma_next = (level_before.astype(jnp.float32) + 1.0) / levels
    updated = latent + (sigma_next - sigma_now) * velocity
    arrived = passed_along(updated.astype(jnp.bfloat16), "queue", -1).astype(updated.dtype)
    queue_next = jnp.where(position == frames - 1, tail_noise, arrived)
    clean_frame = picked(updated.T.astype(jnp.bfloat16), "queue", 0).astype(jnp.float32)
    channel_share = clean_frame.shape[0] // frames
    leaving = lax.dynamic_slice_in_dim(clean_frame, position * channel_share, channel_share, 0)
    return (velocity[None], queue_next[None], leaving)


def dot_nt(a, b):
    return lax.dot_general(a, b, (((1,), (1,)), ((), ())), preferred_element_type=jnp.float32)


def block_kernel(latent_in, mod_in, coef_in, patch_in, qkv_hbm, q_gain_in, k_gain_in, out_hbm,
                 head_hbm, tail_hbm, vel_out, next_out, leaving_out, wide_out,
                 q_in, kv_in, q_all, kv_all, o_send, o_recv, a_send, out,
                 w_buf, ow_buf, hw_buf, tail_buf, hidden_buf, normed_buf, proj_buf,
                 size_buf, u_send, u_recv, lv_send, lv_recv,
                 w_sem, ow_sem, hw_sem, tail_sem, f_s, f_r, u_s, u_r, lv_s, lv_r,
                 xq_s, xq_r, xk_s, xk_r, yq_s, yq_r, zk_s, zk_r, ck_s, ck_r,
                 oy_s, oy_r, ox_s, ox_r):
    queue = lax.axis_index("queue")
    tok = lax.axis_index("tok")
    core = lax.rem(queue, 2)
    z = lax.rem(queue // 2, 4)
    x = (queue // 8) * 2 + tok // 4
    y = lax.rem(tok, 4)

    def device(px, py, pz, pc):
        return (((px // 2) * 4 + pz) * 2 + pc, lax.rem(px, 2) * 4 + py)

    def hop(v, d):
        return lax.rem(v + d + 4, 4)

    slot = z * 2 + core

    def rows(n, size):
        return pl.ds(pl.multiple_of(n * size, size), size)

    def remote(src, dst, s, r, dev):
        return pltpu.make_async_remote_copy(src_ref=src, dst_ref=dst, send_sem=s, recv_sem=r,
                                            device_id=dev, device_id_type=MESH_ID)

    def x_query(h, d):
        g = hop(x, d)
        return remote(q_in.at[g * 3 + h], q_all.at[h, y, rows(x, 128)],
                      xq_s.at[h, d], xq_r.at[h, d], device(g, y, z, core))

    def x_query_in(h, d):
        g = hop(x, -d)
        return remote(q_in.at[x * 3 + h], q_all.at[h, y, rows(g, 128)],
                      xq_s.at[h, d], xq_r.at[h, d], device(g, y, z, core))

    def x_keys(h, d):
        g = hop(x, d)
        return remote(kv_in.at[g * 3 + h], kv_all.at[h, :, rows(slot * 4 + x, 128)],
                      xk_s.at[h, d], xk_r.at[h, d], device(g, y, z, core))

    def x_keys_in(h, d):
        g = hop(x, -d)
        return remote(kv_in.at[x * 3 + h], kv_all.at[h, :, rows(slot * 4 + g, 128)],
                      xk_s.at[h, d], xk_r.at[h, d], device(g, y, z, core))

    def y_query(h, d):
        return remote(q_all.at[h, y], q_all.at[h, y], yq_s.at[h, d], yq_r.at[h, d],
                      device(x, hop(y, d), z, core))

    def y_query_in(h, d):
        g = hop(y, -d)
        return remote(q_all.at[h, g], q_all.at[h, g], yq_s.at[h, d], yq_r.at[h, d],
                      device(x, g, z, core))

    def z_keys(h, d):
        at = kv_all.at[h, :, rows(slot, 512)]
        return remote(at, at, zk_s.at[h, d], zk_r.at[h, d], device(x, y, hop(z, d), core))

    def z_keys_in(h, d):
        g = hop(z, -d)
        at = kv_all.at[h, :, rows(g * 2 + core, 512)]
        return remote(at, at, zk_s.at[h, d], zk_r.at[h, d], device(x, y, g, core))

    def c_keys(h, d):
        at = kv_all.at[h, :, rows(hop(z, -d) * 2 + core, 512)]
        return remote(at, at, ck_s.at[h, d], ck_r.at[h, d], device(x, y, z, 1 - core))

    def c_keys_in(h, d):
        at = kv_all.at[h, :, rows(hop(z, -d) * 2 + 1 - core, 512)]
        return remote(at, at, ck_s.at[h, d], ck_r.at[h, d], device(x, y, z, 1 - core))

    def y_part(h, d):
        return remote(o_send.at[h, hop(y, d)], o_recv.at[h, y], oy_s.at[h, d], oy_r.at[h, d],
                      device(x, hop(y, d), z, core))

    def y_part_in(h, d):
        g = hop(y, -d)
        return remote(o_send.at[h, g], o_recv.at[h, g], oy_s.at[h, d], oy_r.at[h, d],
                      device(x, g, z, core))

    def x_back(h, d):
        g = hop(x, d)
        return remote(a_send.at[h, g], out.at[x * 3 + h], ox_s.at[h, d], ox_r.at[h, d],
                      device(g, y, z, core))

    def x_back_in(h, d):
        g = hop(x, -d)
        return remote(a_send.at[h, g], out.at[g * 3 + h], ox_s.at[h, d], ox_r.at[h, d],
                      device(g, y, z, core))

    def size_step(stage, d, arriving=False):
        if stage == 0:
            dev, src = device(hop(x, d), y, z, core), device(hop(x, -d), y, z, core)
        elif stage == 1:
            dev, src = device(x, y, hop(z, d), core), device(x, y, hop(z, -d), core)
        elif stage == 2:
            dev, src = device(x, hop(y, d), z, core), device(x, hop(y, -d), z, core)
        else:
            dev, src = device(x, y, z, 1 - core), device(x, y, z, 1 - core)
        return remote(size_buf.at[stage, 0], size_buf.at[stage, d],
                      f_s.at[stage, d], f_r.at[stage, d], src if arriving else dev)

    def size_peers(stage):
        return (1, 2, 3) if stage < 3 else (1,)

    def size_send(stage):
        for d in size_peers(stage):
            size_step(stage, d).start()

    def size_take(stage):
        top = size_buf[stage, 0]
        for d in size_peers(stage):
            size_step(stage, d, True).wait_recv()
            top = jnp.maximum(top, size_buf[stage, d])
        return top

    def weight(b):
        return pltpu.make_async_copy(qkv_hbm.at[:, b * 512:(b + 1) * 512], w_buf.at[b],
                                     w_sem.at[b])

    out_copy = pltpu.make_async_copy(out_hbm, ow_buf, ow_sem)
    head_copy = pltpu.make_async_copy(head_hbm, hw_buf, hw_sem)
    tail_copy = pltpu.make_async_copy(tail_hbm, tail_buf, tail_sem)
    for b in (3, 4, 5, 6, 7, 8, 0, 1, 2):
        weight(b).start()
    barrier = pltpu.get_barrier_semaphore()
    for n in range(1, 16):
        pl.semaphore_signal(barrier, inc=1, device_id=(lax.rem(queue + n, 16), tok),
                            device_id_type=MESH_ID)
    for d in (1, 3):
        pl.semaphore_signal(barrier, inc=1, device_id=device(hop(x, d), y, z, core),
                            device_id_type=MESH_ID)
    for d in (1, 2, 3):
        pl.semaphore_signal(barrier, inc=1, device_id=device(x, hop(y, d), z, core),
                            device_id_type=MESH_ID)

    hidden = jnp.dot(latent_in[...].astype(jnp.bfloat16), patch_in[...],
                     preferred_element_type=jnp.float32)
    hidden_buf[...] = hidden
    normed_buf[...] = (layer_norm(hidden) * (1.0 + mod_in[1:2, :]) + mod_in[0:1, :]).astype(
        jnp.bfloat16)

    def project(b, at):
        weight(b).wait()
        part = jnp.dot(normed_buf[...], w_buf[b], preferred_element_type=jnp.float32)
        proj_buf[:, at * 512:(at + 1) * 512] = part
        return jnp.sum(part * part, axis=-1, keepdims=True)

    def pick():
        row = lax.broadcasted_iota(jnp.int32, (1536, 128), 0)
        lane = lax.broadcasted_iota(jnp.int32, (1536, 128), 1)
        return jnp.logical_and(row >= lane * 128, row < lane * 128 + 128).astype(jnp.bfloat16)

    def top_norm(values):
        wide = values.astype(jnp.float32)
        sums = jnp.dot((wide * wide).astype(jnp.bfloat16), pick(),
                       preferred_element_type=jnp.float32)
        return jnp.max(sums, axis=0, keepdims=True) * 1.01

    square = project(3, 0) + project(4, 1) + project(5, 2)
    factor = lax.rsqrt(square * (1.0 / 1536) + 1e-06)
    keys = (proj_buf[...] * factor * k_gain_in[...]).astype(jnp.bfloat16)
    for n in range(12):
        kv_in[n, 0] = keys[:, n * 128:(n + 1) * 128]
    key_size = top_norm(keys)
    top = jnp.zeros((128, 128), jnp.float32)
    for b in range(3):
        weight(6 + b).wait()
        part = jnp.dot(normed_buf[...], w_buf[6 + b], preferred_element_type=jnp.float32)
        part = part * VALUE_SHRINK
        for n in range(4):
            piece = part[:, n * 128:(n + 1) * 128]
            top = jnp.maximum(top, jnp.abs(piece))
            kv_in[b * 4 + n, 1] = piece.astype(jnp.bfloat16)
    value_size = jnp.max(top, axis=0, keepdims=True)

    pl.semaphore_wait(barrier, 20)
    for h in range(3):
        for d in (1, 3, 2):
            x_keys(h, d).start()
        for kv in range(2):
            kv_all[h, kv, rows(slot * 4 + x, 128), :] = kv_in[x * 3 + h, kv]

    square = project(0, 0) + project(1, 1) + project(2, 2)
    out_copy.start()
    head_copy.start()
    tail_copy.start()
    factor = lax.rsqrt(square * (1.0 / 1536) + 1e-06) * (HEAD_DIM ** (-0.5) * LOG2E)
    queries = (proj_buf[...] * factor * q_gain_in[...]).astype(jnp.bfloat16)
    for n in range(12):
        q_in[n] = queries[:, n * 128:(n + 1) * 128]
    for h in range(3):
        for d in (1, 3, 2):
            x_query(h, d).start()
        q_all[h, y, rows(x, 128), :] = q_in[x * 3 + h]
    size_buf[0, 0] = jnp.concatenate(
        [top_norm(queries), key_size, value_size, jnp.zeros((5, 128), jnp.float32)], axis=0)
    size_send(0)

    def spread(h):
        for d in (1, 3, 2):
            x_keys_in(h, d).wait_recv()
        for d in (1, 3, 2):
            z_keys(h, d).start()
        c_keys(h, 0).start()
        for d in (1, 3, 2):
            x_query_in(h, d).wait_recv()
        for d in (1, 3, 2):
            y_query(h, d).start()

    def share(h, d):
        z_keys_in(h, d).wait_recv()
        c_keys(h, d).start()

    for h in range(3):
        spread(h)
    for d in (1, 3, 2):
        share(0, d)
    for d in (0, 1, 3, 2):
        c_keys_in(0, d).wait_recv()

    def combine(h):
        for d in (1, 2, 3):
            y_part_in(h, d).wait_recv()
        parts = [o_send.at[h, y]] + [o_recv.at[h, hop(y, d)] for d in (1, 2, 3)]
        den = jnp.zeros((4, 128), jnp.float32)
        for part in parts:
            tail = part[512:528, :].astype(jnp.float32)
            den = den + (tail[0:4] + tail[4:8])
        inv = (1.0 / VALUE_SHRINK) / den
        for g in range(4):
            num = parts[0][g * 128:(g + 1) * 128, :].astype(jnp.float32)
            for part in parts[1:]:
                num = num + part[g * 128:(g + 1) * 128, :].astype(jnp.float32)
            column = jnp.transpose(jnp.broadcast_to(inv[g:g + 1, :], (128, 128)))
            a_send[h, g] = (num * column).astype(jnp.bfloat16)
        out[x * 3 + h] = a_send[h, x]
        for d in (1, 3, 2):
            x_back(h, d).start()

    def chunk(t, carry):
        h, i = t // 4, lax.rem(t, 4)
        to = lax.rem(y + i + 1, 4)

        @pl.when(i < 3)
        def _():
            y_query_in(h, 3 - i).wait_recv()

        queries = q_all[h, to]
        scores = dot_nt(queries, kv_all[h, 0])
        weights = jnp.exp2(scores)
        total = weights[:, 0:128]
        for n in range(1, 32):
            total = total + weights[:, n * 128:(n + 1) * 128]
        num = jnp.dot(weights.astype(jnp.bfloat16), kv_all[h, 1],
                      preferred_element_type=jnp.float32)
        o_send[h, to, 0:512, :] = num.astype(jnp.bfloat16)
        rows_of = [jnp.sum(jnp.transpose(total[g * 128:(g + 1) * 128, :]), axis=0, keepdims=True)
                   for g in range(4)]
        den = jnp.concatenate(rows_of, axis=0)
        high = den.astype(jnp.bfloat16).astype(jnp.float32)
        tail = jnp.concatenate([high, den - high, jnp.zeros((8, 128), jnp.float32)], axis=0)
        o_send[h, to, 512:528, :] = tail.astype(jnp.bfloat16)

        @pl.when(i < 3)
        def _():
            y_part(h, i + 1).start()

        @pl.when(jnp.logical_and(h < 2, i == 1))
        def _():
            share(h + 1, 1)
            share(h + 1, 3)

        @pl.when(jnp.logical_and(h < 2, i == 2))
        def _():
            share(h + 1, 2)

        @pl.when(jnp.logical_and(h < 2, i == 3))
        def _():
            for d in (0, 1, 3, 2):
                c_keys_in(h + 1, d).wait_recv()

        @pl.when(jnp.logical_and(h > 0, i == 1))
        def _():
            combine(h - 1)

        for stage in range(3):
            @pl.when(t == 2 * stage + 2)
            def _():
                size_buf[stage + 1, 0] = size_take(stage)
                size_send(stage + 1)

        return carry

    lax.fori_loop(0, 12, chunk, 0)
    sizes = size_take(3)
    wide = jnp.maximum(sizes[0:1] * sizes[1:2] - SAFE_LOG2 * SAFE_LOG2, sizes[2:3] - 2.0)
    wide = jnp.max(wide, axis=1, keepdims=True)
    wide_out[...] = jnp.broadcast_to(wide, (8, 128))
    combine(2)
    out_copy.wait()
    head_copy.wait()
    tail_copy.wait()
    for h in range(3):
        for d in (1, 3, 2):
            x_back_in(h, d).wait_recv()
    attended = jnp.concatenate([out[n] for n in range(12)], axis=1)
    attn_out = jnp.dot(attended, ow_buf[...], preferred_element_type=jnp.float32)
    residual = hidden_buf[...] + mod_in[2:3, :] * attn_out
    velocity = jnp.dot(residual.astype(jnp.bfloat16), hw_buf[...],
                       preferred_element_type=jnp.float32)
    vel_out[...] = velocity
    updated = jnp.transpose(latent_in[...] + coef_in[0] * velocity)
    u_send[...] = updated

    send_next = remote(u_send, u_recv, u_s, u_r, (lax.rem(queue + 15, 16), tok))
    take_next = remote(u_send, u_recv, u_s, u_r, (lax.rem(queue + 1, 16), tok))

    def send_leaving(n):
        return remote(lv_send.at[n], lv_recv, lv_s.at[n], lv_r, (n, tok))

    @pl.when(queue > 0)
    def _():
        send_next.start()

    @pl.when(queue == 0)
    def _():
        for n in range(1, 16):
            lv_send[n, 0:4, :] = updated[n * 4:n * 4 + 4, :]
            lv_send[n, 4:8, :] = jnp.zeros((4, 128), jnp.float32)
            send_leaving(n).start()
        leaving_out[...] = updated[0:4, :]

    @pl.when(queue == 15)
    def _():
        next_out[...] = tail_buf[...]

    @pl.when(queue < 15)
    def _():
        take_next.wait_recv()
        next_out[...] = jnp.transpose(u_recv[...])

    @pl.when(queue > 0)
    def _():
        send_leaving(0).wait_recv()
        leaving_out[...] = lv_recv[0:4, :]
        send_next.wait_send()

    @pl.when(queue == 0)
    def _():
        for n in range(1, 16):
            send_leaving(n).wait_send()

    for stage in range(4):
        for d in size_peers(stage):
            size_step(stage, d).wait_send()
    for h in range(3):
        for d in (1, 2, 3):
            x_keys(h, d).wait_send()
            x_query(h, d).wait_send()
            y_query(h, d).wait_send()
            z_keys(h, d).wait_send()
            y_part(h, d).wait_send()
            x_back(h, d).wait_send()
        for d in range(4):
            c_keys(h, d).wait_send()


def block(*operands):
    sems = [pltpu.SemaphoreType.DMA((3, 4))] * 14
    vmem, hbm = pl.BlockSpec(memory_space=pltpu.VMEM), pl.BlockSpec(memory_space=pltpu.HBM)
    smem = pl.BlockSpec(memory_space=pltpu.SMEM)
    f32, bf16, dma = jnp.float32, jnp.bfloat16, pltpu.SemaphoreType.DMA
    return pl.pallas_call(
        block_kernel,
        out_shape=[
            jax.ShapeDtypeStruct((128, 64), f32),
            jax.ShapeDtypeStruct((128, 64), f32),
            jax.ShapeDtypeStruct((4, 128), f32),
            jax.ShapeDtypeStruct((8, 128), f32),
        ],
        in_specs=[vmem, vmem, smem, vmem, hbm, vmem, vmem, hbm, hbm, hbm],
        out_specs=[vmem] * 4,
        scratch_shapes=[
            pltpu.VMEM((12, 128, 128), bf16),
            pltpu.VMEM((12, 2, 128, 128), bf16),
            pltpu.VMEM((3, 4, 512, 128), bf16),
            pltpu.VMEM((3, 2, 4096, 128), bf16),
            pltpu.VMEM((3, 4, 528, 128), bf16),
            pltpu.VMEM((3, 4, 528, 128), bf16),
            pltpu.VMEM((3, 4, 128, 128), bf16),
            pltpu.VMEM((12, 128, 128), bf16),
            pltpu.VMEM((9, 1536, 512), bf16),
            pltpu.VMEM((1536, 1536), bf16),
            pltpu.VMEM((1536, 64), bf16),
            pltpu.VMEM((128, 64), f32),
            pltpu.VMEM((128, 1536), f32),
            pltpu.VMEM((128, 1536), bf16),
            pltpu.VMEM((128, 1536), f32),
            pltpu.VMEM((4, 4, 8, 128), f32),
            pltpu.VMEM((64, 128), f32),
            pltpu.VMEM((64, 128), f32),
            pltpu.VMEM((16, 8, 128), f32),
            pltpu.VMEM((8, 128), f32),
            dma((9,)), dma(()), dma(()), dma(()), dma((4, 4)), dma((4, 4)),
            dma(()), dma(()), dma((16,)), dma(()),
        ] + sems,
        compiler_params=pltpu.CompilerParams(
            collective_id=1, has_side_effects=True, vmem_limit_bytes=58 * 2**20),
        cost_estimate=pl.CostEstimate(flops=16 * 10**9, bytes_accessed=40 * 10**6,
                                      transcendentals=25 * 10**6),
    )(*operands)


def per_device(
    latents,
    step_index,
    tail_noise,
    patch_weight,
    time_table,
    qkv_weight,
    q_gain,
    k_gain,
    out_weight,
    head_weight,
):
    levels = time_table.shape[0]
    position = lax.axis_index("queue")
    level_now = step_index[position]
    level_before = jnp.where(position > 0, step_index[jnp.maximum(position - 1, 0)], -1)
    modulation = lax.dynamic_index_in_dim(time_table, level_now, 0, keepdims=False)
    sigma_now = (level_now.astype(jnp.float32) + 1.0) / levels
    sigma_next = (level_before.astype(jnp.float32) + 1.0) / levels
    velocity, queue_next, leaving, wide = block(
        latents[0], modulation, (sigma_next - sigma_now)[None], patch_weight, qkv_weight,
        q_gain[None], k_gain[None], out_weight, head_weight, tail_noise)
    args = (latents, step_index, tail_noise, patch_weight, time_table, qkv_weight, q_gain,
            k_gain, out_weight, head_weight)
    return lax.cond(wide[0, 0] <= 0.0, lambda *_: (velocity[None], queue_next[None], leaving),
                    careful, *args)


def solution(mesh):
    placed = (P("queue", "tok", None), P(), P("tok", None), P(), P(), P(), P(), P(), P(), P())
    return jax.shard_map(
        per_device,
        mesh=mesh,
        in_specs=placed,
        out_specs=(P("queue", "tok", None), P("queue", "tok", None), P("queue", "tok")),
        check_vma=False,
    )
```

```python
import functools

import jax
import jax.numpy as jnp
from jax import lax
from jax.experimental import pallas as pl
from jax.experimental.pallas import tpu as pltpu
from jax.sharding import PartitionSpec as P

HEAD_DIM = 128
LOG2E = 1.4426950408889634
SAFE_LOG2 = 112.0
VALUE_SHRINK = 0.0625
MESH_ID = pl.DeviceIdType.MESH


def layer_norm(values):
    mean_row = jnp.mean(values, axis=-1, keepdims=True)
    centred = values - mean_row
    variance = jnp.mean(centred * centred, axis=-1, keepdims=True)
    return centred * lax.rsqrt(variance + 1e-06)


def dot_nt(a, b):
    return lax.dot_general(a, b, (((1,), (1,)), ((), ())), preferred_element_type=jnp.float32)


def block_kernel(careful, latent_in, step_in, tail_hbm, patch_in, table_hbm, qkv_hbm, q_gain_in,
                 k_gain_in, out_hbm, head_hbm, vel_out, next_out, leaving_out, wide_out,
                 q_in, kv_in, q_all, kv_all, o_send, o_recv, a_send, out,
                 w_buf, ow_buf, hw_buf, tail_buf, table_buf, hidden_buf, normed_buf, proj_buf,
                 size_buf, u_send, u_recv, lv_send, lv_recv,
                 w_sem, ow_sem, hw_sem, tail_sem, table_sem, f_s, f_r, u_s, u_r, lv_s, lv_r,
                 xq_s, xq_r, xk_s, xk_r, yq_s, yq_r, zk_s, zk_r, ck_s, ck_r,
                 oy_s, oy_r, ox_s, ox_r):
    queue = lax.axis_index("queue")
    tok = lax.axis_index("tok")
    core = lax.rem(queue, 2)
    z = lax.rem(queue // 2, 4)
    x = (queue // 8) * 2 + tok // 4
    y = lax.rem(tok, 4)

    def device(px, py, pz, pc):
        return (((px // 2) * 4 + pz) * 2 + pc, lax.rem(px, 2) * 4 + py)

    def hop(v, d):
        return lax.rem(v + d + 4, 4)

    slot = z * 2 + core

    def rows(n, size):
        return pl.ds(pl.multiple_of(n * size, size), size)

    def remote(src, dst, s, r, dev):
        return pltpu.make_async_remote_copy(src_ref=src, dst_ref=dst, send_sem=s, recv_sem=r,
                                            device_id=dev, device_id_type=MESH_ID)

    def x_query(h, d):
        g = hop(x, d)
        return remote(q_in.at[g * 3 + h], q_all.at[h, y, rows(x, 128)],
                      xq_s.at[h, d], xq_r.at[h, d], device(g, y, z, core))

    def x_query_in(h, d):
        g = hop(x, -d)
        return remote(q_in.at[x * 3 + h], q_all.at[h, y, rows(g, 128)],
                      xq_s.at[h, d], xq_r.at[h, d], device(g, y, z, core))

    def x_keys(h, d):
        g = hop(x, d)
        return remote(kv_in.at[g * 3 + h], kv_all.at[h, :, rows(slot * 4 + x, 128)],
                      xk_s.at[h, d], xk_r.at[h, d], device(g, y, z, core))

    def x_keys_in(h, d):
        g = hop(x, -d)
        return remote(kv_in.at[x * 3 + h], kv_all.at[h, :, rows(slot * 4 + g, 128)],
                      xk_s.at[h, d], xk_r.at[h, d], device(g, y, z, core))

    def y_query(h, d):
        return remote(q_all.at[h, y], q_all.at[h, y], yq_s.at[h, d], yq_r.at[h, d],
                      device(x, hop(y, d), z, core))

    def y_query_in(h, d):
        g = hop(y, -d)
        return remote(q_all.at[h, g], q_all.at[h, g], yq_s.at[h, d], yq_r.at[h, d],
                      device(x, g, z, core))

    def z_keys(h, d):
        at = kv_all.at[h, :, rows(slot, 512)]
        return remote(at, at, zk_s.at[h, d], zk_r.at[h, d], device(x, y, hop(z, d), core))

    def z_keys_in(h, d):
        g = hop(z, -d)
        at = kv_all.at[h, :, rows(g * 2 + core, 512)]
        return remote(at, at, zk_s.at[h, d], zk_r.at[h, d], device(x, y, g, core))

    def c_keys(h, d):
        at = kv_all.at[h, :, rows(hop(z, -d) * 2 + core, 512)]
        return remote(at, at, ck_s.at[h, d], ck_r.at[h, d], device(x, y, z, 1 - core))

    def c_keys_in(h, d):
        at = kv_all.at[h, :, rows(hop(z, -d) * 2 + 1 - core, 512)]
        return remote(at, at, ck_s.at[h, d], ck_r.at[h, d], device(x, y, z, 1 - core))

    def y_part(h, d):
        return remote(o_send.at[h, hop(y, d)], o_recv.at[h, y], oy_s.at[h, d], oy_r.at[h, d],
                      device(x, hop(y, d), z, core))

    def y_part_in(h, d):
        g = hop(y, -d)
        return remote(o_send.at[h, g], o_recv.at[h, g], oy_s.at[h, d], oy_r.at[h, d],
                      device(x, g, z, core))

    def x_back(h, d):
        g = hop(x, d)
        return remote(a_send.at[h, g], out.at[x * 3 + h], ox_s.at[h, d], ox_r.at[h, d],
                      device(g, y, z, core))

    def x_back_in(h, d):
        g = hop(x, -d)
        return remote(a_send.at[h, g], out.at[g * 3 + h], ox_s.at[h, d], ox_r.at[h, d],
                      device(g, y, z, core))

    def size_step(stage, d, arriving=False):
        if stage == 0:
            dev, src = device(hop(x, d), y, z, core), device(hop(x, -d), y, z, core)
        elif stage == 1:
            dev, src = device(x, y, hop(z, d), core), device(x, y, hop(z, -d), core)
        elif stage == 2:
            dev, src = device(x, hop(y, d), z, core), device(x, hop(y, -d), z, core)
        else:
            dev, src = device(x, y, z, 1 - core), device(x, y, z, 1 - core)
        return remote(size_buf.at[stage, 0], size_buf.at[stage, d],
                      f_s.at[stage, d], f_r.at[stage, d], src if arriving else dev)

    def size_peers(stage):
        return (1, 2, 3) if stage < 3 else (1,)

    def size_send(stage):
        for d in size_peers(stage):
            size_step(stage, d).start()

    def size_take(stage):
        top = size_buf[stage, 0]
        for d in size_peers(stage):
            size_step(stage, d, True).wait_recv()
            top = jnp.maximum(top, size_buf[stage, d])
        return top

    def weight(b):
        return pltpu.make_async_copy(qkv_hbm.at[:, b * 512:(b + 1) * 512], w_buf.at[b],
                                     w_sem.at[b])

    out_copy = pltpu.make_async_copy(out_hbm, ow_buf, ow_sem)
    head_copy = pltpu.make_async_copy(head_hbm, hw_buf, hw_sem)
    tail_copy = pltpu.make_async_copy(tail_hbm, tail_buf, tail_sem)
    table_copy = pltpu.make_async_copy(table_hbm, table_buf, table_sem)
    weight(3).start()
    table_copy.start()
    for b in (4, 5, 6, 7, 8, 0, 1, 2):
        weight(b).start()
    barrier = pltpu.get_barrier_semaphore()
    for n in range(1, 16):
        pl.semaphore_signal(barrier, inc=1, device_id=(lax.rem(queue + n, 16), tok),
                            device_id_type=MESH_ID)
    for d in (1, 3):
        pl.semaphore_signal(barrier, inc=1, device_id=device(hop(x, d), y, z, core),
                            device_id_type=MESH_ID)
    for d in (1, 2, 3):
        pl.semaphore_signal(barrier, inc=1, device_id=device(x, hop(y, d), z, core),
                            device_id_type=MESH_ID)

    level_now = step_in[queue]
    level_before = jnp.where(queue > 0, step_in[jnp.maximum(queue - 1, 0)], -1)
    step = (level_before - level_now).astype(jnp.float32) * (1.0 / 64)
    hidden = lax.dot_general(latent_in[...].astype(jnp.bfloat16), patch_in[...],
                             (((0,), (0,)), ((), ())), preferred_element_type=jnp.float32)
    hidden_buf[...] = hidden
    table_copy.wait()
    shift, scale, gate = [table_buf[n, pl.ds(level_now, 1), :] for n in range(3)]
    normed_buf[...] = (layer_norm(hidden) * (1.0 + scale) + shift).astype(jnp.bfloat16)

    def project(b, at):
        weight(b).wait()
        part = jnp.dot(normed_buf[...], w_buf[b], preferred_element_type=jnp.float32)
        proj_buf[:, at * 512:(at + 1) * 512] = part
        return jnp.sum(part * part, axis=-1, keepdims=True)

    def pick():
        row = lax.broadcasted_iota(jnp.int32, (1536, 128), 0)
        lane = lax.broadcasted_iota(jnp.int32, (1536, 128), 1)
        return jnp.logical_and(row >= lane * 128, row < lane * 128 + 128).astype(jnp.bfloat16)

    def top_norm(values):
        wide = values.astype(jnp.float32)
        sums = jnp.dot((wide * wide).astype(jnp.bfloat16), pick(),
                       preferred_element_type=jnp.float32)
        return jnp.max(sums, axis=0, keepdims=True) * 1.01

    square = project(3, 0) + project(4, 1) + project(5, 2)
    factor = lax.rsqrt(square * (1.0 / 1536) + 1e-06)
    keys = (proj_buf[...] * factor * k_gain_in[...].reshape(1, 1536)).astype(jnp.bfloat16)
    for n in range(12):
        kv_in[n, 0] = keys[:, n * 128:(n + 1) * 128]
    key_size = top_norm(keys)
    top = jnp.zeros((128, 128), jnp.float32)
    for b in range(3):
        weight(6 + b).wait()
        part = jnp.dot(normed_buf[...], w_buf[6 + b], preferred_element_type=jnp.float32)
        part = part * VALUE_SHRINK
        for n in range(4):
            piece = part[:, n * 128:(n + 1) * 128]
            top = jnp.maximum(top, jnp.abs(piece))
            kv_in[b * 4 + n, 1] = piece.astype(jnp.bfloat16)
    value_size = jnp.max(top, axis=0, keepdims=True)

    pl.semaphore_wait(barrier, 20)
    for h in range(3):
        for d in (1, 3, 2):
            x_keys(h, d).start()
        for kv in range(2):
            kv_all[h, kv, rows(slot * 4 + x, 128), :] = kv_in[x * 3 + h, kv]

    square = project(0, 0) + project(1, 1) + project(2, 2)
    out_copy.start()
    head_copy.start()
    tail_copy.start()
    factor = lax.rsqrt(square * (1.0 / 1536) + 1e-06) * (HEAD_DIM ** (-0.5) * LOG2E)
    queries = (proj_buf[...] * factor * q_gain_in[...].reshape(1, 1536)).astype(jnp.bfloat16)
    for n in range(12):
        q_in[n] = queries[:, n * 128:(n + 1) * 128]
    for h in range(3):
        for d in (1, 3, 2):
            x_query(h, d).start()
        q_all[h, y, rows(x, 128), :] = q_in[x * 3 + h]
    size_buf[0, 0] = jnp.concatenate(
        [top_norm(queries), key_size, value_size, jnp.zeros((5, 128), jnp.float32)], axis=0)
    size_send(0)

    def spread(h):
        for d in (1, 3, 2):
            x_keys_in(h, d).wait_recv()
        for d in (1, 3, 2):
            z_keys(h, d).start()
        c_keys(h, 0).start()
        for d in (1, 3, 2):
            x_query_in(h, d).wait_recv()
        for d in (1, 3, 2):
            y_query(h, d).start()

    def share(h, d):
        z_keys_in(h, d).wait_recv()
        c_keys(h, d).start()

    for h in range(3):
        spread(h)
    for d in (1, 3, 2):
        share(0, d)
    for d in (0, 1, 3, 2):
        c_keys_in(0, d).wait_recv()

    def combine(h):
        for d in (1, 2, 3):
            y_part_in(h, d).wait_recv()
        parts = [o_send.at[h, y]] + [o_recv.at[h, hop(y, d)] for d in (1, 2, 3)]
        tails = [part[512:528, :].astype(jnp.float32) for part in parts]
        dens = [tail[0:4] + tail[4:8] for tail in tails]
        if careful:
            tops = [tail[8:12] + tail[12:16] for tail in tails]
            top = functools.reduce(jnp.maximum, tops)
            factors = [jnp.exp2(own - top) for own in tops]
            dens = [den * factor for den, factor in zip(dens, factors)]
        inv = (1.0 / VALUE_SHRINK) / (dens[0] + dens[1] + dens[2] + dens[3])

        def column(values, g):
            return jnp.transpose(jnp.broadcast_to(values[g:g + 1, :], (128, 128)))

        for g in range(4):
            nums = [part[g * 128:(g + 1) * 128, :].astype(jnp.float32) for part in parts]
            if careful:
                nums = [num * column(factor, g) for num, factor in zip(nums, factors)]
            num = (nums[0] + nums[1]) + (nums[2] + nums[3])
            a_send[h, g] = (num * column(inv, g)).astype(jnp.bfloat16)
        out[x * 3 + h] = a_send[h, x]
        for d in (1, 3, 2):
            x_back(h, d).start()

    def chunk(t, carry):
        h, i = t // 4, lax.rem(t, 4)
        to = lax.rem(y + i + 1, 4)

        @pl.when(i < 3)
        def _():
            y_query_in(h, 3 - i).wait_recv()

        queries = q_all[h, to]
        scores = dot_nt(queries, kv_all[h, 0])

        def lanes(values, op):
            return functools.reduce(op, [values[:, n * 128:(n + 1) * 128] for n in range(32)])

        def as_rows(values, op):
            return jnp.concatenate(
                [op(jnp.transpose(values[g * 128:(g + 1) * 128, :]), axis=0, keepdims=True)
                 for g in range(4)], axis=0)

        if careful:
            most = lanes(scores, jnp.maximum)
            scores = scores - jnp.ceil(jnp.max(most, axis=1, keepdims=True))
            top = jnp.ceil(as_rows(most, jnp.max))
        else:
            top = jnp.zeros((4, 128), jnp.float32)
        weights = jnp.exp2(scores)
        den = as_rows(lanes(weights, jnp.add), jnp.sum)
        num = jnp.dot(weights.astype(jnp.bfloat16), kv_all[h, 1],
                      preferred_element_type=jnp.float32)
        o_send[h, to, 0:512, :] = num.astype(jnp.bfloat16)

        def two(values):
            high = values.astype(jnp.bfloat16).astype(jnp.float32)
            return [high, values - high]

        tail = jnp.concatenate(two(den) + two(top), axis=0)
        o_send[h, to, 512:528, :] = tail.astype(jnp.bfloat16)

        @pl.when(i < 3)
        def _():
            y_part(h, i + 1).start()

        @pl.when(jnp.logical_and(h < 2, i == 1))
        def _():
            share(h + 1, 1)
            share(h + 1, 3)

        @pl.when(jnp.logical_and(h < 2, i == 2))
        def _():
            share(h + 1, 2)

        @pl.when(jnp.logical_and(h < 2, i == 3))
        def _():
            for d in (0, 1, 3, 2):
                c_keys_in(h + 1, d).wait_recv()

        @pl.when(jnp.logical_and(h > 0, i == 1))
        def _():
            combine(h - 1)

        for stage in range(3):
            @pl.when(t == 2 * stage + 2)
            def _():
                size_buf[stage + 1, 0] = size_take(stage)
                size_send(stage + 1)

        return carry

    lax.fori_loop(0, 12, chunk, 0)
    sizes = size_take(3)
    wide = jnp.maximum(sizes[0:1] * sizes[1:2] - SAFE_LOG2 * SAFE_LOG2, sizes[2:3] - 2.0)
    wide_out[0] = jnp.where(jnp.max(wide) > 0.0, 1, 0)
    combine(2)
    out_copy.wait()
    head_copy.wait()
    tail_copy.wait()
    for h in range(3):
        for d in (1, 3, 2):
            x_back_in(h, d).wait_recv()
    attended = jnp.concatenate([out[n] for n in range(12)], axis=1)
    attn_out = jnp.dot(attended, ow_buf[...], preferred_element_type=jnp.float32)
    residual = hidden_buf[...] + table_buf[2, pl.ds(level_now, 1), :] * attn_out
    velocity = dot_nt(hw_buf[...], residual.astype(jnp.bfloat16))
    vel_out[...] = velocity
    updated = latent_in[...] + step * velocity
    u_send[...] = updated

    send_next = remote(u_send, u_recv, u_s, u_r, (lax.rem(queue + 15, 16), tok))
    take_next = remote(u_send, u_recv, u_s, u_r, (lax.rem(queue + 1, 16), tok))

    def send_leaving(n):
        return remote(lv_send.at[n], lv_recv, lv_s.at[n], lv_r, (n, tok))

    @pl.when(queue > 0)
    def _():
        send_next.start()

    @pl.when(queue == 0)
    def _():
        for n in range(1, 16):
            lv_send[n, 0:4, :] = updated[n * 4:n * 4 + 4, :]
            lv_send[n, 4:8, :] = jnp.zeros((4, 128), jnp.float32)
            send_leaving(n).start()
        leaving_out[...] = updated[0:4, :]

    @pl.when(queue == 15)
    def _():
        next_out[...] = tail_buf[...]

    @pl.when(queue < 15)
    def _():
        take_next.wait_recv()
        next_out[...] = u_recv[...]

    @pl.when(queue > 0)
    def _():
        send_leaving(0).wait_recv()
        leaving_out[...] = lv_recv[0:4, :]
        send_next.wait_send()

    @pl.when(queue == 0)
    def _():
        for n in range(1, 16):
            send_leaving(n).wait_send()

    for stage in range(4):
        for d in size_peers(stage):
            size_step(stage, d).wait_send()
    for h in range(3):
        for d in (1, 2, 3):
            x_keys(h, d).wait_send()
            x_query(h, d).wait_send()
            y_query(h, d).wait_send()
            z_keys(h, d).wait_send()
            y_part(h, d).wait_send()
            x_back(h, d).wait_send()
        for d in range(4):
            c_keys(h, d).wait_send()


def block(careful, *operands):
    sems = [pltpu.SemaphoreType.DMA((3, 4))] * 14
    vmem, hbm = pl.BlockSpec(memory_space=pltpu.VMEM), pl.BlockSpec(memory_space=pltpu.HBM)
    smem = pl.BlockSpec(memory_space=pltpu.SMEM)
    f32, bf16, dma = jnp.float32, jnp.bfloat16, pltpu.SemaphoreType.DMA
    return pl.pallas_call(
        functools.partial(block_kernel, careful),
        out_shape=[
            jax.ShapeDtypeStruct((64, 128), f32),
            jax.ShapeDtypeStruct((64, 128), f32),
            jax.ShapeDtypeStruct((4, 128), f32),
            jax.ShapeDtypeStruct((1,), jnp.int32),
        ],
        in_specs=[vmem, smem, hbm, vmem, hbm, hbm, vmem, vmem, hbm, hbm],
        out_specs=[vmem, vmem, vmem, smem],
        scratch_shapes=[
            pltpu.VMEM((12, 128, 128), bf16),
            pltpu.VMEM((12, 2, 128, 128), bf16),
            pltpu.VMEM((3, 4, 512, 128), bf16),
            pltpu.VMEM((3, 2, 4096, 128), bf16),
            pltpu.VMEM((3, 4, 528, 128), bf16),
            pltpu.VMEM((3, 4, 528, 128), bf16),
            pltpu.VMEM((3, 4, 128, 128), bf16),
            pltpu.VMEM((12, 128, 128), bf16),
            pltpu.VMEM((9, 1536, 512), bf16),
            pltpu.VMEM((1536, 1536), bf16),
            pltpu.VMEM((64, 1536), bf16),
            pltpu.VMEM((64, 128), f32),
            pltpu.VMEM((3, 64, 1536), f32),
            pltpu.VMEM((128, 1536), f32),
            pltpu.VMEM((128, 1536), bf16),
            pltpu.VMEM((128, 1536), f32),
            pltpu.VMEM((4, 4, 8, 128), f32),
            pltpu.VMEM((64, 128), f32),
            pltpu.VMEM((64, 128), f32),
            pltpu.VMEM((16, 8, 128), f32),
            pltpu.VMEM((8, 128), f32),
            dma((9,)), dma(()), dma(()), dma(()), dma(()), dma((4, 4)), dma((4, 4)),
            dma(()), dma(()), dma((16,)), dma(()),
        ] + sems,
        compiler_params=pltpu.CompilerParams(
            collective_id=2 if careful else 1, has_side_effects=True, vmem_limit_bytes=58 * 2**20),
        cost_estimate=pl.CostEstimate(flops=16 * 10**9, bytes_accessed=40 * 10**6,
                                      transcendentals=25 * 10**6),
    )(*operands)


def per_device(
    latents,
    step_index,
    tail_noise,
    patch_weight,
    time_table,
    qkv_weight,
    q_gain,
    k_gain,
    out_weight,
    head_weight,
):
    operands = (latents[0].T, step_index, tail_noise.T, patch_weight,
                time_table.transpose(1, 0, 2), qkv_weight, q_gain, k_gain, out_weight,
                head_weight.T)
    *fast, wide = block(False, *operands)
    velocity, queue_next, leaving = lax.cond(
        wide[0] == 0, lambda *_: tuple(fast), lambda *a: tuple(block(True, *a)[:3]), *operands)
    return velocity.T[None], queue_next.T[None], leaving


def solution(mesh):
    placed = (P("queue", "tok", None), P(), P("tok", None), P(), P(), P(), P(), P(), P(), P())
    return jax.shard_map(
        per_device,
        mesh=mesh,
        in_specs=placed,
        out_specs=(P("queue", "tok", None), P("queue", "tok", None), P("queue", "tok")),
        check_vma=False,
    )
```

```python
import functools

import jax
import jax.numpy as jnp
from jax import lax
from jax.experimental import pallas as pl
from jax.experimental.pallas import tpu as pltpu
from jax.sharding import PartitionSpec as P

HEAD_DIM = 128
LOG2E = 1.4426950408889634
SAFE_LOG2 = 112.0
VALUE_SHRINK = 0.0625
MESH_ID = pl.DeviceIdType.MESH


def layer_norm(values):
    mean_row = jnp.mean(values, axis=-1, keepdims=True)
    centred = values - mean_row
    variance = jnp.mean(centred * centred, axis=-1, keepdims=True)
    return centred * lax.rsqrt(variance + 1e-06)


def dot_nt(a, b):
    return lax.dot_general(a, b, (((1,), (1,)), ((), ())), preferred_element_type=jnp.float32)


def block_kernel(careful, latent_in, step_in, tail_hbm, patch_in, table_hbm, qkv_hbm, q_gain_in,
                 k_gain_in, out_hbm, head_hbm, vel_out, next_out, leaving_out, wide_out,
                 q_in, kv_in, q_all, kv_all, o_send, o_recv, a_send, out,
                 w_buf, ow_buf, hw_buf, tail_buf, table_buf, hidden_buf, normed_buf, proj_buf, num_buf, den_buf,
                 size_buf, u_send, u_recv, lv_send, lv_recv,
                 w_sem, ow_sem, hw_sem, tail_sem, table_sem, f_s, f_r, u_s, u_r, lv_s, lv_r,
                 xq_s, xq_r, xk_s, xk_r, yq_s, yq_r, zk_s, zk_r, ck_s, ck_r,
                 oy_s, oy_r, ox_s, ox_r):
    queue = lax.axis_index("queue")
    tok = lax.axis_index("tok")
    core = lax.rem(queue, 2)
    z = lax.rem(queue // 2, 4)
    x = (queue // 8) * 2 + tok // 4
    y = lax.rem(tok, 4)

    def device(px, py, pz, pc):
        return (((px // 2) * 4 + pz) * 2 + pc, lax.rem(px, 2) * 4 + py)

    def hop(v, d):
        return lax.rem(v + d + 4, 4)

    def rows(n, size):
        return pl.ds(pl.multiple_of(n * size, size), size)

    def coordinate(axis):
        if isinstance(axis, int):
            return (x, y, z)[axis]
        return jnp.where(axis == 0, x, jnp.where(axis == 1, y, z))

    def turned(h, by):
        return (h + by) % 3 if isinstance(h, int) else lax.rem(h + by, 3)

    def peer(axis, d):
        at = hop(coordinate(axis), d)
        if isinstance(axis, int):
            return device(*[at if axis == n else v for n, v in enumerate((x, y, z))], core)
        return device(*[jnp.where(axis == n, at, v) for n, v in enumerate((x, y, z))], core)

    place = {0: 0, 1: 1, 3: 2, 2: 3}

    def remote(src, dst, s, r, dev):
        return pltpu.make_async_remote_copy(src_ref=src, dst_ref=dst, send_sem=s, recv_sem=r,
                                            device_id=dev, device_id_type=MESH_ID)

    def x_query(h, d):
        mine = coordinate(h)
        return remote(q_in.at[hop(mine, d) * 3 + h], q_all.at[h, 0, rows(mine, 128)],
                      xq_s.at[h, d], xq_r.at[h, d], peer(h, d))

    def x_query_in(h, d):
        mine = coordinate(h)
        return remote(q_in.at[mine * 3 + h], q_all.at[h, 0, rows(hop(mine, -d), 128)],
                      xq_s.at[h, d], xq_r.at[h, d], peer(h, -d))

    def x_keys(h, d):
        mine = coordinate(h)
        return remote(kv_in.at[hop(mine, d) * 3 + h], kv_all.at[h, :, rows(core * 4 + mine, 128)],
                      xk_s.at[h, d], xk_r.at[h, d], peer(h, d))

    def x_keys_in(h, d):
        mine = coordinate(h)
        return remote(kv_in.at[mine * 3 + h],
                      kv_all.at[h, :, rows(core * 4 + hop(mine, -d), 128)],
                      xk_s.at[h, d], xk_r.at[h, d], peer(h, -d))

    def y_query(h, d, arriving=False):
        return remote(q_all.at[h, 0], q_all.at[h, 4 - d], yq_s.at[h, d], yq_r.at[h, d],
                      peer(turned(h, 1), -d if arriving else d))

    def key_place(h, d, half):
        return kv_all.at[h, :, rows(place[(4 - d) % 4] * 2 + half, 512)]

    def z_keys(h, d, arriving=False):
        return remote(key_place(h, 0, core), key_place(h, d, core), zk_s.at[h, d],
                      zk_r.at[h, d], peer(turned(h, 2), -d if arriving else d))

    def c_keys(h, d, arriving=False):
        at = key_place(h, d, 1 - core if arriving else core)
        return remote(at, at, ck_s.at[h, d], ck_r.at[h, d], device(x, y, z, 1 - core))

    def y_part(h, d, arriving=False):
        return remote(o_send.at[h, d], o_recv.at[h, 4 - d], oy_s.at[h, d], oy_r.at[h, d],
                      peer(turned(h, 1), -d if arriving else d))

    def x_back(h, d):
        mine = coordinate(h)
        return remote(a_send.at[h, hop(mine, d)], out.at[mine * 3 + h],
                      ox_s.at[h, d], ox_r.at[h, d], peer(h, d))

    def x_back_in(h, d):
        mine = coordinate(h)
        return remote(a_send.at[h, hop(mine, -d)], out.at[hop(mine, -d) * 3 + h],
                      ox_s.at[h, d], ox_r.at[h, d], peer(h, -d))

    def size_step(stage, d, arriving=False):
        if stage == 0:
            dev, src = device(hop(x, d), y, z, core), device(hop(x, -d), y, z, core)
        elif stage == 1:
            dev, src = device(x, y, hop(z, d), core), device(x, y, hop(z, -d), core)
        elif stage == 2:
            dev, src = device(x, hop(y, d), z, core), device(x, hop(y, -d), z, core)
        else:
            dev, src = device(x, y, z, 1 - core), device(x, y, z, 1 - core)
        return remote(size_buf.at[stage, 0], size_buf.at[stage, d],
                      f_s.at[stage, d], f_r.at[stage, d], src if arriving else dev)

    def size_peers(stage):
        return (1, 2, 3) if stage < 3 else (1,)

    def size_send(stage):
        for d in size_peers(stage):
            size_step(stage, d).start()

    def size_take(stage):
        top = size_buf[stage, 0]
        for d in size_peers(stage):
            size_step(stage, d, True).wait_recv()
            top = jnp.maximum(top, size_buf[stage, d])
        return top

    def weight(b):
        return pltpu.make_async_copy(qkv_hbm.at[:, b * 512:(b + 1) * 512], w_buf.at[b],
                                     w_sem.at[b])

    out_copy = pltpu.make_async_copy(out_hbm, ow_buf, ow_sem)
    head_copy = pltpu.make_async_copy(head_hbm, hw_buf, hw_sem)
    tail_copy = pltpu.make_async_copy(tail_hbm, tail_buf, tail_sem)
    table_copy = pltpu.make_async_copy(table_hbm, table_buf, table_sem)
    weight(3).start()
    table_copy.start()
    for b in (4, 5, 6, 7, 8, 0, 1, 2):
        weight(b).start()
    barrier = pltpu.get_barrier_semaphore()
    for n in range(1, 16):
        pl.semaphore_signal(barrier, inc=1, device_id=(lax.rem(queue + n, 16), tok),
                            device_id_type=MESH_ID)
    for d in (1, 3):
        pl.semaphore_signal(barrier, inc=1, device_id=device(hop(x, d), y, z, core),
                            device_id_type=MESH_ID)
    for d in (1, 2, 3):
        pl.semaphore_signal(barrier, inc=1, device_id=device(x, hop(y, d), z, core),
                            device_id_type=MESH_ID)

    level_now = step_in[queue]
    level_before = jnp.where(queue > 0, step_in[jnp.maximum(queue - 1, 0)], -1)
    step = (level_before - level_now).astype(jnp.float32) * (1.0 / 64)
    hidden = lax.dot_general(latent_in[...].astype(jnp.bfloat16), patch_in[...],
                             (((0,), (0,)), ((), ())), preferred_element_type=jnp.float32)
    hidden_buf[...] = hidden
    table_copy.wait()
    shift, scale, gate = [table_buf[n, pl.ds(level_now, 1), :] for n in range(3)]
    normed_buf[...] = (layer_norm(hidden) * (1.0 + scale) + shift).astype(jnp.bfloat16)

    def project(b, at):
        weight(b).wait()
        part = jnp.dot(normed_buf[...], w_buf[b], preferred_element_type=jnp.float32)
        proj_buf[:, at * 512:(at + 1) * 512] = part
        return jnp.sum(part * part, axis=-1, keepdims=True)

    def pick():
        row = lax.broadcasted_iota(jnp.int32, (1536, 128), 0)
        lane = lax.broadcasted_iota(jnp.int32, (1536, 128), 1)
        return jnp.logical_and(row >= lane * 128, row < lane * 128 + 128).astype(jnp.bfloat16)

    def top_norm(values):
        wide = values.astype(jnp.float32)
        sums = jnp.dot((wide * wide).astype(jnp.bfloat16), pick(),
                       preferred_element_type=jnp.float32)
        return jnp.max(sums, axis=0, keepdims=True) * 1.01

    square = project(3, 0) + project(4, 1) + project(5, 2)
    factor = lax.rsqrt(square * (1.0 / 1536) + 1e-06)
    keys = (proj_buf[...] * factor * k_gain_in[...].reshape(1, 1536)).astype(jnp.bfloat16)
    for n in range(12):
        kv_in[n, 0] = keys[:, n * 128:(n + 1) * 128]
    key_size = top_norm(keys)
    top = jnp.zeros((128, 128), jnp.float32)
    for b in range(3):
        weight(6 + b).wait()
        part = jnp.dot(normed_buf[...], w_buf[6 + b], preferred_element_type=jnp.float32)
        part = part * VALUE_SHRINK
        for n in range(4):
            piece = part[:, n * 128:(n + 1) * 128]
            top = jnp.maximum(top, jnp.abs(piece))
            kv_in[b * 4 + n, 1] = piece.astype(jnp.bfloat16)
    value_size = jnp.max(top, axis=0, keepdims=True)

    pl.semaphore_wait(barrier, 20)
    for h in range(3):
        for d in (1, 3, 2):
            x_keys(h, d).start()
    for h in range(3):
        mine = coordinate(h)
        for kv in range(2):
            kv_all[h, kv, rows(core * 4 + mine, 128), :] = kv_in[mine * 3 + h, kv]

    square = project(0, 0) + project(1, 1) + project(2, 2)
    out_copy.start()
    head_copy.start()
    tail_copy.start()
    factor = lax.rsqrt(square * (1.0 / 1536) + 1e-06) * (HEAD_DIM ** (-0.5) * LOG2E)
    queries = (proj_buf[...] * factor * q_gain_in[...].reshape(1, 1536)).astype(jnp.bfloat16)
    for n in range(12):
        q_in[n] = queries[:, n * 128:(n + 1) * 128]
    for h in range(3):
        for d in (1, 3, 2):
            x_query(h, d).start()
        q_all[h, 0, rows(coordinate(h), 128), :] = q_in[coordinate(h) * 3 + h]
    size_buf[0, 0] = jnp.concatenate(
        [top_norm(queries), key_size, value_size, jnp.zeros((5, 128), jnp.float32)], axis=0)
    size_send(0)

    def spread_keys(h):
        for d in (1, 3, 2):
            x_keys_in(h, d).wait_recv()
        for d in (1, 3):
            z_keys(h, d).start()
        c_keys(h, 0).start()
        z_keys(h, 2).start()

    def spread_queries(h):
        for d in (1, 3, 2):
            x_query_in(h, d).wait_recv()
        for d in (1, 3, 2):
            y_query(h, d).start()

    def share(h, *steps):
        for d in steps:
            z_keys(h, d, True).wait_recv()
            c_keys(h, d).start()

    def shared(h, *steps):
        for d in steps:
            c_keys(h, d, True).wait_recv()

    spread_keys(0)
    spread_keys(1)
    spread_queries(0)
    spread_keys(2)
    spread_queries(1)
    spread_queries(2)
    share(0, 1, 3)
    shared(0, 0, 1, 3)

    def combine(h):
        for d in (1, 2, 3):
            y_part(h, d, True).wait_recv()
        parts = [o_send.at[h, 0]] + [o_recv.at[h, d] for d in (1, 2, 3)]
        mine = coordinate(h)
        tails = [part[512:528, :].astype(jnp.float32) for part in parts]
        dens = [tail[0:4] + tail[4:8] for tail in tails]
        if careful:
            tops = [tail[8:12] + tail[12:16] for tail in tails]
            top = functools.reduce(jnp.maximum, tops)
            factors = [jnp.exp2(own - top) for own in tops]
            dens = [den * factor for den, factor in zip(dens, factors)]
        inv = (1.0 / VALUE_SHRINK) / (dens[0] + dens[1] + dens[2] + dens[3])

        def column(values, g):
            return jnp.transpose(jnp.broadcast_to(values[g:g + 1, :], (128, 128)))

        for g in range(4):
            nums = [part[g * 128:(g + 1) * 128, :].astype(jnp.float32) for part in parts]
            if careful:
                nums = [num * column(factor, g) for num, factor in zip(nums, factors)]
            num = (nums[0] + nums[1]) + (nums[2] + nums[3])
            a_send[h, g] = (num * column(inv, g)).astype(jnp.bfloat16)
        out[mine * 3 + h] = a_send[h, mine]
        for d in (1, 3, 2):
            x_back(h, d).start()

    def lanes(values, op):
        return functools.reduce(op, [values[:, n:n + 128] for n in range(0, values.shape[1], 128)])

    def as_rows(values, op):
        return jnp.concatenate(
            [op(jnp.transpose(values[g * 128:(g + 1) * 128, :]), axis=0, keepdims=True)
             for g in range(4)], axis=0)

    def two(values):
        high = values.astype(jnp.bfloat16).astype(jnp.float32)
        return [high, values - high]

    def fold(h, at, first, last):
        scores = dot_nt(q_all[h, at], kv_all[h, 0, first:last, :])
        top = jnp.zeros((4, 128), jnp.float32)
        if careful:
            most = lanes(scores, jnp.maximum)
            scores = scores - jnp.ceil(jnp.max(most, axis=1, keepdims=True))
            top = jnp.ceil(as_rows(most, jnp.max))
        weights = jnp.exp2(scores)
        num = jnp.dot(weights.astype(jnp.bfloat16), kv_all[h, 1, first:last, :],
                      preferred_element_type=jnp.float32)
        return num, lanes(weights, jnp.add), top

    def write_part(h, at, num, den, top):
        o_send[h, at, 0:512, :] = num.astype(jnp.bfloat16)
        tail = jnp.concatenate(two(as_rows(den, jnp.sum)) + two(top), axis=0)
        o_send[h, at, 512:528, :] = tail.astype(jnp.bfloat16)

    def early(at, carry):
        for d in (1, 2, 3):
            @pl.when(at == 4 - d)
            def _():
                y_query(0, d, True).wait_recv()

        if not careful:
            num, den, _ = fold(0, at, 0, 3072)
            num_buf[at] = num
            den_buf[at] = den

        @pl.when(at == 1)
        def _():
            share(0, 2)

        @pl.when(at == 2)
        def _():
            share(1, 1, 3)

        @pl.when(at == 3)
        def _():
            share(1, 2)

        return carry

    lax.fori_loop(0, 4, early, 0)
    shared(0, 2)

    def chunk(t, carry):
        h, i = t // 4, lax.rem(t, 4)
        at = lax.rem(i + 1, 4)

        @pl.when(jnp.logical_and(h > 0, i < 3))
        def _():
            y_query(h, 3 - i, True).wait_recv()

        if careful:
            write_part(h, at, *fold(h, at, 0, 4096))
        else:
            @pl.when(h == 0)
            def _():
                num, den, top = fold(0, at, 3072, 4096)
                write_part(0, at, num_buf[at] + num, den_buf[at] + den, top)

            @pl.when(h > 0)
            def _():
                write_part(h, at, *fold(h, at, 0, 4096))

        @pl.when(i < 3)
        def _():
            y_part(h, i + 1).start()

        @pl.when(t == 0)
        def _():
            share(2, 1, 3)

        @pl.when(t == 1)
        def _():
            share(2, 2)

        for own in (1, 2):
            @pl.when(t == own * 4 - 1)
            def _():
                shared(own, 0, 1, 3, 2)

        @pl.when(jnp.logical_and(h > 0, i == 1))
        def _():
            combine(h - 1)

        for stage in range(3):
            @pl.when(t == 2 * stage + 2)
            def _():
                size_buf[stage + 1, 0] = size_take(stage)
                size_send(stage + 1)

        return carry

    lax.fori_loop(0, 12, chunk, 0)
    sizes = size_take(3)
    wide = jnp.maximum(sizes[0:1] * sizes[1:2] - SAFE_LOG2 * SAFE_LOG2, sizes[2:3] - 2.0)
    wide_out[0] = jnp.where(jnp.max(wide) > 0.0, 1, 0)
    combine(2)
    out_copy.wait()
    head_copy.wait()
    tail_copy.wait()
    for h in range(2):
        for d in (1, 3, 2):
            x_back_in(h, d).wait_recv()
    attn_out = jnp.zeros((128, 1536), jnp.float32)
    for g in range(4):
        pair = jnp.concatenate([out[g * 3], out[g * 3 + 1]], axis=1)
        attn_out = attn_out + jnp.dot(pair, ow_buf[g * 384:g * 384 + 256, :],
                                      preferred_element_type=jnp.float32)
    proj_buf[...] = attn_out
    for d in (1, 3, 2):
        x_back_in(2, d).wait_recv()
    last = jnp.concatenate([out[g * 3 + 2] for g in range(4)], axis=1)
    last_weight = jnp.concatenate(
        [ow_buf[g * 384 + 256:g * 384 + 384, :] for g in range(4)], axis=0)
    attn_out = proj_buf[...] + jnp.dot(last, last_weight, preferred_element_type=jnp.float32)
    residual = hidden_buf[...] + table_buf[2, pl.ds(level_now, 1), :] * attn_out
    velocity = dot_nt(hw_buf[...], residual.astype(jnp.bfloat16))
    vel_out[...] = velocity
    updated = latent_in[...] + step * velocity
    u_send[...] = updated

    send_next = remote(u_send, u_recv, u_s, u_r, (lax.rem(queue + 15, 16), tok))
    take_next = remote(u_send, u_recv, u_s, u_r, (lax.rem(queue + 1, 16), tok))

    def send_leaving(n):
        return remote(lv_send.at[n], lv_recv, lv_s.at[n], lv_r, (n, tok))

    @pl.when(queue > 0)
    def _():
        send_next.start()

    @pl.when(queue == 0)
    def _():
        for n in range(1, 16):
            lv_send[n, 0:4, :] = updated[n * 4:n * 4 + 4, :]
            lv_send[n, 4:8, :] = jnp.zeros((4, 128), jnp.float32)
            send_leaving(n).start()
        leaving_out[...] = updated[0:4, :]

    @pl.when(queue == 15)
    def _():
        next_out[...] = tail_buf[...]

    @pl.when(queue < 15)
    def _():
        take_next.wait_recv()
        next_out[...] = u_recv[...]

    @pl.when(queue > 0)
    def _():
        send_leaving(0).wait_recv()
        leaving_out[...] = lv_recv[0:4, :]
        send_next.wait_send()

    @pl.when(queue == 0)
    def _():
        for n in range(1, 16):
            send_leaving(n).wait_send()

    for stage in range(4):
        for d in size_peers(stage):
            size_step(stage, d).wait_send()
    for h in range(3):
        for d in (1, 2, 3):
            x_keys(h, d).wait_send()
            x_query(h, d).wait_send()
            y_query(h, d).wait_send()
            z_keys(h, d).wait_send()
            y_part(h, d).wait_send()
            x_back(h, d).wait_send()
        for d in range(4):
            c_keys(h, d).wait_send()


def block(careful, *operands):
    sems = [pltpu.SemaphoreType.DMA((3, 4))] * 14
    vmem, hbm = pl.BlockSpec(memory_space=pltpu.VMEM), pl.BlockSpec(memory_space=pltpu.HBM)
    smem = pl.BlockSpec(memory_space=pltpu.SMEM)
    f32, bf16, dma = jnp.float32, jnp.bfloat16, pltpu.SemaphoreType.DMA
    return pl.pallas_call(
        functools.partial(block_kernel, careful),
        out_shape=[
            jax.ShapeDtypeStruct((64, 128), f32),
            jax.ShapeDtypeStruct((64, 128), f32),
            jax.ShapeDtypeStruct((4, 128), f32),
            jax.ShapeDtypeStruct((1,), jnp.int32),
        ],
        in_specs=[vmem, smem, hbm, vmem, hbm, hbm, vmem, vmem, hbm, hbm],
        out_specs=[vmem, vmem, vmem, smem],
        scratch_shapes=[
            pltpu.VMEM((12, 128, 128), bf16),
            pltpu.VMEM((12, 2, 128, 128), bf16),
            pltpu.VMEM((3, 4, 512, 128), bf16),
            pltpu.VMEM((3, 2, 4096, 128), bf16),
            pltpu.VMEM((3, 4, 528, 128), bf16),
            pltpu.VMEM((3, 4, 528, 128), bf16),
            pltpu.VMEM((3, 4, 128, 128), bf16),
            pltpu.VMEM((12, 128, 128), bf16),
            pltpu.VMEM((9, 1536, 512), bf16),
            pltpu.VMEM((1536, 1536), bf16),
            pltpu.VMEM((64, 1536), bf16),
            pltpu.VMEM((64, 128), f32),
            pltpu.VMEM((3, 64, 1536), f32),
            pltpu.VMEM((128, 1536), f32),
            pltpu.VMEM((128, 1536), bf16),
            pltpu.VMEM((128, 1536), f32),
            pltpu.VMEM((4, 512, 128), f32),
            pltpu.VMEM((4, 512, 128), f32),
            pltpu.VMEM((4, 4, 8, 128), f32),
            pltpu.VMEM((64, 128), f32),
            pltpu.VMEM((64, 128), f32),
            pltpu.VMEM((16, 8, 128), f32),
            pltpu.VMEM((8, 128), f32),
            dma((9,)), dma(()), dma(()), dma(()), dma(()), dma((4, 4)), dma((4, 4)),
            dma(()), dma(()), dma((16,)), dma(()),
        ] + sems,
        compiler_params=pltpu.CompilerParams(
            collective_id=2 if careful else 1, has_side_effects=True, vmem_limit_bytes=58 * 2**20),
        cost_estimate=pl.CostEstimate(flops=16 * 10**9, bytes_accessed=40 * 10**6,
                                      transcendentals=25 * 10**6),
    )(*operands)


def per_device(
    latents,
    step_index,
    tail_noise,
    patch_weight,
    time_table,
    qkv_weight,
    q_gain,
    k_gain,
    out_weight,
    head_weight,
):
    operands = (latents[0].T, step_index, tail_noise.T, patch_weight,
                time_table.transpose(1, 0, 2), qkv_weight, q_gain, k_gain, out_weight,
                head_weight.T)
    *fast, wide = block(False, *operands)
    velocity, queue_next, leaving = lax.cond(
        wide[0] == 0, lambda *_: tuple(fast), lambda *a: tuple(block(True, *a)[:3]), *operands)
    return velocity.T[None], queue_next.T[None], leaving


def solution(mesh):
    placed = (P("queue", "tok", None), P(), P("tok", None), P(), P(), P(), P(), P(), P(), P())
    return jax.shard_map(
        per_device,
        mesh=mesh,
        in_specs=placed,
        out_specs=(P("queue", "tok", None), P("queue", "tok", None), P("queue", "tok")),
        check_vma=False,
    )
```

```python
import functools

import jax
import jax.numpy as jnp
from jax import lax
from jax.experimental import pallas as pl
from jax.experimental.pallas import tpu as pltpu
from jax.sharding import PartitionSpec as P

HEAD_DIM = 128
LOG2E = 1.4426950408889634
SAFE_LOG2 = 112.0
VALUE_SHRINK = 0.0625
MESH_ID = pl.DeviceIdType.MESH


def layer_norm(values):
    mean_row = jnp.mean(values, axis=-1, keepdims=True)
    centred = values - mean_row
    variance = jnp.mean(centred * centred, axis=-1, keepdims=True)
    return centred * lax.rsqrt(variance + 1e-06)


def dot_nt(a, b):
    return lax.dot_general(a, b, (((1,), (1,)), ((), ())), preferred_element_type=jnp.float32)


def block_kernel(careful, latent_in, step_in, tail_hbm, patch_in, table_hbm, qkv_hbm, q_gain_in,
                 k_gain_in, out_hbm, head_hbm, vel_out, next_out, leaving_out, wide_out,
                 q_in, kv_in, q_all, kv_all, o_send, o_recv, a_send, out,
                 w_buf, ow_buf, hw_buf, tail_buf, table_buf, hidden_buf, normed_buf, proj_buf, num_buf, den_buf,
                 size_buf, u_send, u_recv, lv_send, lv_recv,
                 w_sem, ow_sem, hw_sem, tail_sem, table_sem, f_s, f_r, u_s, u_r, lv_s, lv_r,
                 xq_s, xq_r, xk_s, xk_r, yq_s, yq_r, zk_s, zk_r, ck_s, ck_r,
                 oy_s, oy_r, ox_s, ox_r):
    queue = lax.axis_index("queue")
    tok = lax.axis_index("tok")
    core = lax.rem(queue, 2)
    z = lax.rem(queue // 2, 4)
    x = (queue // 8) * 2 + tok // 4
    y = lax.rem(tok, 4)

    def device(px, py, pz, pc):
        return (((px // 2) * 4 + pz) * 2 + pc, lax.rem(px, 2) * 4 + py)

    def hop(v, d):
        return lax.rem(v + d + 4, 4)

    def rows(n, size):
        return pl.ds(pl.multiple_of(n * size, size), size)

    def coordinate(axis):
        if isinstance(axis, int):
            return (x, y, z)[axis]
        return jnp.where(axis == 0, x, jnp.where(axis == 1, y, z))

    def turned(h, by):
        return (h + by) % 3 if isinstance(h, int) else lax.rem(h + by, 3)

    def peer(axis, d):
        at = hop(coordinate(axis), d)
        if isinstance(axis, int):
            return device(*[at if axis == n else v for n, v in enumerate((x, y, z))], core)
        return device(*[jnp.where(axis == n, at, v) for n, v in enumerate((x, y, z))], core)

    place = {0: 0, 1: 1, 3: 2, 2: 3}

    def remote(src, dst, s, r, dev):
        return pltpu.make_async_remote_copy(src_ref=src, dst_ref=dst, send_sem=s, recv_sem=r,
                                            device_id=dev, device_id_type=MESH_ID)

    def x_query(h, d):
        mine = coordinate(h)
        return remote(q_in.at[hop(mine, d) * 3 + h], q_all.at[h, 0, rows(mine, 128)],
                      xq_s.at[h, d], xq_r.at[h, d], peer(h, d))

    def x_query_in(h, d):
        mine = coordinate(h)
        return remote(q_in.at[mine * 3 + h], q_all.at[h, 0, rows(hop(mine, -d), 128)],
                      xq_s.at[h, d], xq_r.at[h, d], peer(h, -d))

    def x_keys(h, d, kv):
        mine = coordinate(h)
        return remote(kv_in.at[kv, hop(mine, d) * 3 + h],
                      kv_all.at[h, kv, rows(core * 4 + mine, 128)],
                      xk_s.at[kv, h, d], xk_r.at[kv, h, d], peer(h, d))

    def x_keys_in(h, d, kv):
        mine = coordinate(h)
        return remote(kv_in.at[kv, mine * 3 + h],
                      kv_all.at[h, kv, rows(core * 4 + hop(mine, -d), 128)],
                      xk_s.at[kv, h, d], xk_r.at[kv, h, d], peer(h, -d))

    def y_query(h, d, arriving=False):
        return remote(q_all.at[h, 0], q_all.at[h, 4 - d], yq_s.at[h, d], yq_r.at[h, d],
                      peer(turned(h, 1), -d if arriving else d))

    def key_place(h, d, kv, half):
        return kv_all.at[h, kv, rows(place[(4 - d) % 4] * 2 + half, 512)]

    def z_keys(h, d, kv, arriving=False):
        return remote(key_place(h, 0, kv, core), key_place(h, d, kv, core), zk_s.at[kv, h, d],
                      zk_r.at[kv, h, d], peer(turned(h, 2), -d if arriving else d))

    def c_keys(h, d, kv, arriving=False):
        at = key_place(h, d, kv, 1 - core if arriving else core)
        return remote(at, at, ck_s.at[kv, h, d], ck_r.at[kv, h, d], device(x, y, z, 1 - core))

    def y_part(h, d, arriving=False):
        return remote(o_send.at[h, d], o_recv.at[h, 4 - d], oy_s.at[h, d], oy_r.at[h, d],
                      peer(turned(h, 1), -d if arriving else d))

    def x_back(h, d):
        mine = coordinate(h)
        return remote(a_send.at[h, hop(mine, d)], out.at[mine * 3 + h],
                      ox_s.at[h, d], ox_r.at[h, d], peer(h, d))

    def x_back_in(h, d):
        mine = coordinate(h)
        return remote(a_send.at[h, hop(mine, -d)], out.at[hop(mine, -d) * 3 + h],
                      ox_s.at[h, d], ox_r.at[h, d], peer(h, -d))

    def size_step(stage, d, arriving=False):
        if stage == 0:
            dev, src = device(hop(x, d), y, z, core), device(hop(x, -d), y, z, core)
        elif stage == 1:
            dev, src = device(x, y, hop(z, d), core), device(x, y, hop(z, -d), core)
        elif stage == 2:
            dev, src = device(x, hop(y, d), z, core), device(x, hop(y, -d), z, core)
        else:
            dev, src = device(x, y, z, 1 - core), device(x, y, z, 1 - core)
        return remote(size_buf.at[stage, 0], size_buf.at[stage, d],
                      f_s.at[stage, d], f_r.at[stage, d], src if arriving else dev)

    def size_peers(stage):
        return (1, 2, 3) if stage < 3 else (1,)

    def size_send(stage):
        for d in size_peers(stage):
            size_step(stage, d).start()

    def size_take(stage):
        top = size_buf[stage, 0]
        for d in size_peers(stage):
            size_step(stage, d, True).wait_recv()
            top = jnp.maximum(top, size_buf[stage, d])
        return top

    def weight(b):
        return pltpu.make_async_copy(qkv_hbm.at[:, b * 512:(b + 1) * 512], w_buf.at[b],
                                     w_sem.at[b])

    out_copy = pltpu.make_async_copy(out_hbm, ow_buf, ow_sem)
    head_copy = pltpu.make_async_copy(head_hbm, hw_buf, hw_sem)
    tail_copy = pltpu.make_async_copy(tail_hbm, tail_buf, tail_sem)
    table_copy = pltpu.make_async_copy(table_hbm, table_buf, table_sem)
    weight(3).start()
    table_copy.start()
    for b in (4, 5, 0, 1, 2, 6, 7, 8):
        weight(b).start()
    barrier = pltpu.get_barrier_semaphore()
    for n in range(1, 16):
        pl.semaphore_signal(barrier, inc=1, device_id=(lax.rem(queue + n, 16), tok),
                            device_id_type=MESH_ID)
    for d in (1, 3):
        pl.semaphore_signal(barrier, inc=1, device_id=device(hop(x, d), y, z, core),
                            device_id_type=MESH_ID)
    for d in (1, 2, 3):
        pl.semaphore_signal(barrier, inc=1, device_id=device(x, hop(y, d), z, core),
                            device_id_type=MESH_ID)

    level_now = step_in[queue]
    level_before = jnp.where(queue > 0, step_in[jnp.maximum(queue - 1, 0)], -1)
    step = (level_before - level_now).astype(jnp.float32) * (1.0 / 64)
    hidden = lax.dot_general(latent_in[...].astype(jnp.bfloat16), patch_in[...],
                             (((0,), (0,)), ((), ())), preferred_element_type=jnp.float32)
    hidden_buf[...] = hidden
    table_copy.wait()
    shift, scale, gate = [table_buf[n, pl.ds(level_now, 1), :] for n in range(3)]
    normed_buf[...] = (layer_norm(hidden) * (1.0 + scale) + shift).astype(jnp.bfloat16)

    def project(b, at):
        weight(b).wait()
        part = jnp.dot(normed_buf[...], w_buf[b], preferred_element_type=jnp.float32)
        proj_buf[:, at * 512:(at + 1) * 512] = part
        return jnp.sum(part * part, axis=-1, keepdims=True)

    def top_norm(heads):
        lane = lax.broadcasted_iota(jnp.int32, (1, 128), 1)
        row = jnp.zeros((1, 128), jnp.float32)
        for n in range(12):
            wide = heads[n].astype(jnp.float32)
            most = jnp.max(jnp.sum(wide * wide, axis=-1, keepdims=True), axis=0, keepdims=True)
            row = jnp.where(lane == n, most, row)
        return row * 1.01

    def scatter_keys(kv):
        for d in (1, 3, 2):
            for h in range(3):
                x_keys(h, d, kv).start()
        for h in range(3):
            mine = coordinate(h)
            kv_all[h, kv, rows(core * 4 + mine, 128), :] = kv_in[kv, mine * 3 + h]

    def spread_keys(h, kv):
        for d in (1, 3, 2):
            x_keys_in(h, d, kv).wait_recv()
        for d in (1, 3):
            z_keys(h, d, kv).start()
        c_keys(h, 0, kv).start()
        z_keys(h, 2, kv).start()

    def spread_queries(h):
        for d in (1, 3, 2):
            x_query_in(h, d).wait_recv()
        for d in (1, 3, 2):
            y_query(h, d).start()

    def share(h, *steps):
        for kv in range(2):
            for d in steps:
                z_keys(h, d, kv, True).wait_recv()
                c_keys(h, d, kv).start()

    def shared(h, *steps):
        for kv in range(2):
            for d in steps:
                c_keys(h, d, kv, True).wait_recv()

    square = project(3, 0) + project(4, 1) + project(5, 2)
    factor = lax.rsqrt(square * (1.0 / 1536) + 1e-06)
    keys = (proj_buf[...] * factor * k_gain_in[...].reshape(1, 1536)).astype(jnp.bfloat16)
    for n in range(12):
        kv_in[0, n] = keys[:, n * 128:(n + 1) * 128]
    pl.semaphore_wait(barrier, 20)
    scatter_keys(0)

    square = project(0, 0) + project(1, 1) + project(2, 2)
    factor = lax.rsqrt(square * (1.0 / 1536) + 1e-06) * (HEAD_DIM ** (-0.5) * LOG2E)
    queries = (proj_buf[...] * factor * q_gain_in[...].reshape(1, 1536)).astype(jnp.bfloat16)
    for n in range(12):
        q_in[n] = queries[:, n * 128:(n + 1) * 128]
    for d in (1, 3, 2):
        for h in range(3):
            x_query(h, d).start()
    for h in range(3):
        q_all[h, 0, rows(coordinate(h), 128), :] = q_in[coordinate(h) * 3 + h]
    for h in range(3):
        spread_keys(h, 0)

    for b in range(3):
        weight(6 + b).wait()
        part = jnp.dot(normed_buf[...], w_buf[6 + b], preferred_element_type=jnp.float32)
        part = (part * VALUE_SHRINK).astype(jnp.bfloat16)
        for n in range(4):
            kv_in[1, b * 4 + n] = part[:, n * 128:(n + 1) * 128]
    out_copy.start()
    head_copy.start()
    tail_copy.start()
    scatter_keys(1)
    for h in range(3):
        spread_queries(h)

    top = functools.reduce(jnp.maximum, [jnp.abs(kv_in[1, n].astype(jnp.float32))
                                         for n in range(12)])
    size_buf[0, 0] = jnp.concatenate(
        [top_norm(q_in[...]), top_norm(kv_in[0]), jnp.max(top, axis=0, keepdims=True),
         jnp.zeros((5, 128), jnp.float32)], axis=0)
    for h in range(3):
        spread_keys(h, 1)
    size_send(0)

    def combine(h):
        for d in (1, 2, 3):
            y_part(h, d, True).wait_recv()
        parts = [o_send.at[h, 0]] + [o_recv.at[h, d] for d in (1, 2, 3)]
        mine = coordinate(h)
        tails = [part[512:528, :].astype(jnp.float32) for part in parts]
        dens = [tail[0:4] + tail[4:8] for tail in tails]
        if careful:
            tops = [tail[8:12] + tail[12:16] for tail in tails]
            top = functools.reduce(jnp.maximum, tops)
            factors = [jnp.exp2(own - top) for own in tops]
            dens = [den * factor for den, factor in zip(dens, factors)]
        inv = (1.0 / VALUE_SHRINK) / (dens[0] + dens[1] + dens[2] + dens[3])

        def column(values, g):
            return jnp.transpose(jnp.broadcast_to(values[g:g + 1, :], (128, 128)))

        for g in range(4):
            nums = [part[g * 128:(g + 1) * 128, :].astype(jnp.float32) for part in parts]
            if careful:
                nums = [num * column(factor, g) for num, factor in zip(nums, factors)]
            num = (nums[0] + nums[1]) + (nums[2] + nums[3])
            a_send[h, g] = (num * column(inv, g)).astype(jnp.bfloat16)
        out[mine * 3 + h] = a_send[h, mine]
        for d in (1, 3, 2):
            x_back(h, d).start()

    def lanes(values, op):
        return functools.reduce(op, [values[:, n:n + 128] for n in range(0, values.shape[1], 128)])

    def as_rows(values, op):
        return jnp.concatenate(
            [op(jnp.transpose(values[g * 128:(g + 1) * 128, :]), axis=0, keepdims=True)
             for g in range(4)], axis=0)

    def two(values):
        high = values.astype(jnp.bfloat16).astype(jnp.float32)
        return [high, values - high]

    def fold(h, at, first, last):
        scores = dot_nt(q_all[h, at], kv_all[h, 0, first:last, :])
        top = jnp.zeros((4, 128), jnp.float32)
        if careful:
            most = lanes(scores, jnp.maximum)
            scores = scores - jnp.ceil(jnp.max(most, axis=1, keepdims=True))
            top = jnp.ceil(as_rows(most, jnp.max))
        weights = jnp.exp2(scores)
        num = jnp.dot(weights.astype(jnp.bfloat16), kv_all[h, 1, first:last, :],
                      preferred_element_type=jnp.float32)
        return num, lanes(weights, jnp.add), top

    def write_part(h, at, num, den, top):
        o_send[h, at, 0:512, :] = num.astype(jnp.bfloat16)
        tail = jnp.concatenate(two(as_rows(den, jnp.sum)) + two(top), axis=0)
        o_send[h, at, 512:528, :] = tail.astype(jnp.bfloat16)

    def early(e, carry):
        r, h = e // 3, lax.rem(e, 3)
        at = r + r // 2

        @pl.when(r == 0)
        def _():
            shared(h, 0)

        @pl.when(r > 0)
        def _():
            y_query(h, 4 - at, True).wait_recv()

        if not careful:
            num, den, _ = fold(h, at, 0, 1024)
            num_buf[h, at] = num
            den_buf[h, at] = den

        @pl.when(e == 6)
        def _():
            share(0, 1, 3)

        @pl.when(e == 7)
        def _():
            share(1, 1, 3)

        return carry

    lax.fori_loop(0, 9, early, 0)
    share(0, 2)
    shared(0, 1, 3, 2)

    def chunk(t, carry):
        h = jnp.where(t < 4, 0, jnp.where(t < 10, (t - 1) // 3, t - 9))
        i = jnp.where(t < 4, t, jnp.where(t < 10, lax.rem(t - 1, 3), 3))
        at = lax.rem(i + 1, 4)

        @pl.when(at == 2)
        def _():
            y_query(h, 2, True).wait_recv()

        if careful:
            write_part(h, at, *fold(h, at, 0, 4096))
        else:
            @pl.when(at == 2)
            def _():
                write_part(h, at, *fold(h, at, 0, 4096))

            @pl.when(at != 2)
            def _():
                num, den, top = fold(h, at, 1024, 4096)
                write_part(h, at, num_buf[h, at] + num, den_buf[h, at] + den, top)

        @pl.when(i < 3)
        def _():
            y_part(h, i + 1).start()

        @pl.when(t == 0)
        def _():
            share(1, 2)
            share(2, 1, 3)

        @pl.when(t == 1)
        def _():
            share(2, 2)

        for own in (1, 2):
            @pl.when(t == own * 3)
            def _():
                shared(own, 1, 3, 2)

            @pl.when(t == own * 5)
            def _():
                combine(own - 1)

        for stage in range(3):
            @pl.when(t == 2 * stage + 2)
            def _():
                size_buf[stage + 1, 0] = size_take(stage)
                size_send(stage + 1)

        return carry

    lax.fori_loop(0, 12, chunk, 0)
    sizes = size_take(3)
    wide = jnp.maximum(sizes[0:1] * sizes[1:2] - SAFE_LOG2 * SAFE_LOG2, sizes[2:3] - 2.0)
    wide_out[0] = jnp.where(jnp.max(wide) > 0.0, 1, 0)
    combine(2)
    out_copy.wait()
    head_copy.wait()
    tail_copy.wait()
    for h in range(2):
        for d in (1, 3, 2):
            x_back_in(h, d).wait_recv()
    attn_out = jnp.zeros((128, 1536), jnp.float32)
    for g in range(4):
        pair = jnp.concatenate([out[g * 3], out[g * 3 + 1]], axis=1)
        attn_out = attn_out + jnp.dot(pair, ow_buf[g * 384:g * 384 + 256, :],
                                      preferred_element_type=jnp.float32)
    proj_buf[...] = attn_out
    for d in (1, 3, 2):
        x_back_in(2, d).wait_recv()
    last = jnp.concatenate([out[g * 3 + 2] for g in range(4)], axis=1)
    last_weight = jnp.concatenate(
        [ow_buf[g * 384 + 256:g * 384 + 384, :] for g in range(4)], axis=0)
    attn_out = proj_buf[...] + jnp.dot(last, last_weight, preferred_element_type=jnp.float32)
    residual = hidden_buf[...] + table_buf[2, pl.ds(level_now, 1), :] * attn_out
    velocity = dot_nt(hw_buf[...], residual.astype(jnp.bfloat16))
    vel_out[...] = velocity
    updated = latent_in[...] + step * velocity
    u_send[...] = updated

    send_next = remote(u_send, u_recv, u_s, u_r, (lax.rem(queue + 15, 16), tok))
    take_next = remote(u_send, u_recv, u_s, u_r, (lax.rem(queue + 1, 16), tok))

    def send_leaving(n):
        return remote(lv_send.at[n], lv_recv, lv_s.at[n], lv_r, (n, tok))

    @pl.when(queue > 0)
    def _():
        send_next.start()

    @pl.when(queue == 0)
    def _():
        for n in range(1, 16):
            lv_send[n, 0:4, :] = updated[n * 4:n * 4 + 4, :]
            lv_send[n, 4:8, :] = jnp.zeros((4, 128), jnp.float32)
            send_leaving(n).start()
        leaving_out[...] = updated[0:4, :]

    @pl.when(queue == 15)
    def _():
        next_out[...] = tail_buf[...]

    @pl.when(queue < 15)
    def _():
        take_next.wait_recv()
        next_out[...] = u_recv[...]

    @pl.when(queue > 0)
    def _():
        send_leaving(0).wait_recv()
        leaving_out[...] = lv_recv[0:4, :]
        send_next.wait_send()

    @pl.when(queue == 0)
    def _():
        for n in range(1, 16):
            send_leaving(n).wait_send()

    for stage in range(4):
        for d in size_peers(stage):
            size_step(stage, d).wait_send()
    for h in range(3):
        for d in (1, 2, 3):
            for kv in range(2):
                x_keys(h, d, kv).wait_send()
                z_keys(h, d, kv).wait_send()
            x_query(h, d).wait_send()
            y_query(h, d).wait_send()
            y_part(h, d).wait_send()
            x_back(h, d).wait_send()
        for d in range(4):
            for kv in range(2):
                c_keys(h, d, kv).wait_send()


def block(careful, *operands):
    one, both = pltpu.SemaphoreType.DMA((3, 4)), pltpu.SemaphoreType.DMA((2, 3, 4))
    sems = [one] * 2 + [both] * 2 + [one] * 2 + [both] * 4 + [one] * 4
    vmem, hbm = pl.BlockSpec(memory_space=pltpu.VMEM), pl.BlockSpec(memory_space=pltpu.HBM)
    smem = pl.BlockSpec(memory_space=pltpu.SMEM)
    f32, bf16, dma = jnp.float32, jnp.bfloat16, pltpu.SemaphoreType.DMA
    return pl.pallas_call(
        functools.partial(block_kernel, careful),
        out_shape=[
            jax.ShapeDtypeStruct((64, 128), f32),
            jax.ShapeDtypeStruct((64, 128), f32),
            jax.ShapeDtypeStruct((4, 128), f32),
            jax.ShapeDtypeStruct((1,), jnp.int32),
        ],
        in_specs=[vmem, smem, hbm, vmem, hbm, hbm, vmem, vmem, hbm, hbm],
        out_specs=[vmem, vmem, vmem, smem],
        scratch_shapes=[
            pltpu.VMEM((12, 128, 128), bf16),
            pltpu.VMEM((2, 12, 128, 128), bf16),
            pltpu.VMEM((3, 4, 512, 128), bf16),
            pltpu.VMEM((3, 2, 4096, 128), bf16),
            pltpu.VMEM((3, 4, 528, 128), bf16),
            pltpu.VMEM((3, 4, 528, 128), bf16),
            pltpu.VMEM((3, 4, 128, 128), bf16),
            pltpu.VMEM((12, 128, 128), bf16),
            pltpu.VMEM((9, 1536, 512), bf16),
            pltpu.VMEM((1536, 1536), bf16),
            pltpu.VMEM((64, 1536), bf16),
            pltpu.VMEM((64, 128), f32),
            pltpu.VMEM((3, 64, 1536), f32),
            pltpu.VMEM((128, 1536), f32),
            pltpu.VMEM((128, 1536), bf16),
            pltpu.VMEM((128, 1536), f32),
            pltpu.VMEM((3, 4, 512, 128), f32),
            pltpu.VMEM((3, 4, 512, 128), f32),
            pltpu.VMEM((4, 4, 8, 128), f32),
            pltpu.VMEM((64, 128), f32),
            pltpu.VMEM((64, 128), f32),
            pltpu.VMEM((16, 8, 128), f32),
            pltpu.VMEM((8, 128), f32),
            dma((9,)), dma(()), dma(()), dma(()), dma(()), dma((4, 4)), dma((4, 4)),
            dma(()), dma(()), dma((16,)), dma(()),
        ] + sems,
        compiler_params=pltpu.CompilerParams(
            collective_id=2 if careful else 1, has_side_effects=True, vmem_limit_bytes=58 * 2**20),
        cost_estimate=pl.CostEstimate(flops=16 * 10**9, bytes_accessed=40 * 10**6,
                                      transcendentals=25 * 10**6),
    )(*operands)


def per_device(
    latents,
    step_index,
    tail_noise,
    patch_weight,
    time_table,
    qkv_weight,
    q_gain,
    k_gain,
    out_weight,
    head_weight,
):
    operands = (latents[0].T, step_index, tail_noise.T, patch_weight,
                time_table.transpose(1, 0, 2), qkv_weight, q_gain, k_gain, out_weight,
                head_weight.T)
    *fast, wide = block(False, *operands)
    velocity, queue_next, leaving = lax.cond(
        wide[0] == 0, lambda *_: tuple(fast), lambda *a: tuple(block(True, *a)[:3]), *operands)
    return velocity.T[None], queue_next.T[None], leaving


def solution(mesh):
    placed = (P("queue", "tok", None), P(), P("tok", None), P(), P(), P(), P(), P(), P(), P())
    return jax.shard_map(
        per_device,
        mesh=mesh,
        in_specs=placed,
        out_specs=(P("queue", "tok", None), P("queue", "tok", None), P("queue", "tok")),
        check_vma=False,
    )
```
